256 devices in a mesh: ctx: 16 (over x_lo, z), head: 16 (over y, x_hi, core).
Axes of the slice: x: 4 (x_hi: 2, x_lo: 2; x = x_hi * 2 + x_lo), y: 4, z: 8, core: 2. Of those that a mesh axis runs over, the one named last changes fastest.
Arguments:
- queries: bfloat16 [1536, 6144], P('ctx', 'head'), may hold values from -120 to 120
- new_keys: bfloat16 [1536, 6144], P('ctx', 'head'), may hold values from -4 to 4
- new_values: bfloat16 [1536, 6144], P('ctx', 'head'), may hold values from -5 to 5
- cache_keys: bfloat16 [32768, 6144], P('ctx', 'head'), may hold values from -4 to 4
- cache_values: bfloat16 [32768, 6144], P('ctx', 'head'), may hold values from -5 to 5
- out_weight: bfloat16 [6144, 6144], P('head'), may hold values from -0.109375 to 0.109375
Outputs:
- mixed: float32 [1536, 6144], P('ctx', 'head')
The draws below stay inside these ranges and needn't reach their ends.
All inputs are finite; a program needn't handle non-finite values.
Results may differ from the reference program's by a relative error of at most 0.006.
Values may be sent and summed in bfloat16 or wider, within the bound.
No kernel may reach another device: no remote copies, remote signals or barrier semaphores. Data moves between devices by JAX's collectives and lax.ppermute only.
A program may use at most 128 MiB of HBM per device.

```python
import jax
import jax.numpy as jnp
from jax import lax

D = 6144
HD = 128
HEADS = 48
QROWS = 1536
CACHE = 32768


def shared_keys(key):
    return jnp.clip(jax.random.normal(key, (CACHE, HEADS * HD), jnp.float32), -4.0, 4.0)


def draw_cache_keys(key, part):
    common = shared_keys(key)
    return common.astype(jnp.bfloat16)


def draw_queries(key, part):
    key = jax.random.fold_in(key, 23)
    result = 3.0 * jnp.clip(jax.random.normal(key, (QROWS, HEADS * HD), jnp.float32), -4.0, 4.0)
    return result.astype(jnp.bfloat16)


def spiked(drawn, key, source, target, blocks, factor):
    owner, partner = [(jnp.arange(drawn.shape[position]) // (drawn.shape[position] // blocks)).reshape([-1 if axis == position else 1 for axis in range(drawn.ndim)]) for position in (source, target)]
    chosen = jax.random.permutation(key, blocks)[partner]
    strong = (owner == chosen) | (owner == (partner + blocks // 2) % blocks)
    return jnp.where(strong, factor * drawn, drawn)


def block_scale(own_key, shape, cuts, low, top_value):
    def one(axis_at, parts):
        steps = jax.random.uniform(jax.random.fold_in(jax.random.fold_in(own_key, 6), axis_at), (parts,), jnp.float32, low / len(cuts), top_value / len(cuts))
        return jnp.repeat(jnp.exp(steps), shape[axis_at] // parts).reshape((-1,) + (1,) * (len(shape) - axis_at - 1))

    gain = one(*cuts[0])
    for cut in cuts[1:]:
        gain = gain * one(*cut)
    return gain


def scatter_about(key, dims, scale, most, pieces=(), kind=jnp.bfloat16):
    values = scale * jax.random.normal(key, dims, jnp.float32)
    if pieces:
        values = values * block_scale(key, dims, pieces, -0.22, 0.18)
    return jnp.clip(values, -most, most).astype(kind)


def heavy_noise(key, dims, deviation, limit, pieces, heavy, dtype=jnp.bfloat16):
    entries = deviation * jax.random.normal(key, dims, jnp.float32)
    if pieces:
        entries = entries * block_scale(key, dims, pieces, -0.22, 0.18)
    return jnp.clip(spiked(entries, jax.random.fold_in(key, 3), *heavy), -limit, limit).astype(dtype)


def setup_inputs(seed: int = 0) -> dict:
    key_of = jax.random.split(jax.random.key(seed), 7)
    queries = draw_queries(jax.random.fold_in(key_of[6], 71), 0)
    new_keys = scatter_about(key_of[1], (QROWS, HEADS * HD), 1.0, 4.0, ((0, 16), (1, 16)))
    new_values = scatter_about(key_of[2], (QROWS, HEADS * HD), 1.0, 5.0, ((0, 16), (1, 16)))
    cache_keys = draw_cache_keys(jax.random.fold_in(key_of[6], 71), 0)
    cache_values = scatter_about(key_of[4], (CACHE, HEADS * HD), 1.0, 5.0, ((0, 16), (1, 16)))
    out_weight = heavy_noise(key_of[5], (HEADS * HD, D), (HEADS * HD) ** -0.5, 0.109375, ((0, 16),), (0, 1, 16, 2.0))
    return dict(queries=queries, new_keys=new_keys, new_values=new_values, cache_keys=cache_keys, cache_values=cache_values, out_weight=out_weight)


def one_head(operands):
    query_part, key_part, value_part = operands
    scores = jnp.dot(query_part, key_part.T, preferred_element_type=jnp.float32) * (HD ** -0.5)
    highest = jnp.max(scores, axis=1, keepdims=True)
    weights = jnp.exp(scores - highest)
    totals = jnp.sum(weights, axis=1, keepdims=True)
    summed = jnp.dot(weights.astype(jnp.bfloat16), value_part, preferred_element_type=jnp.float32)
    return summed / totals


def reference(queries, new_keys, new_values, cache_keys, cache_values, out_weight):
    all_keys = jnp.concatenate([cache_keys, new_keys], axis=0)
    all_values = jnp.concatenate([cache_values, new_values], axis=0)
    head_queries = queries.reshape(QROWS, HEADS, HD).transpose(1, 0, 2)
    head_keys = all_keys.reshape(-1, HEADS, HD).transpose(1, 0, 2)
    head_values = all_values.reshape(-1, HEADS, HD).transpose(1, 0, 2)
    outputs = lax.map(one_head, (head_queries, head_keys, head_values))
    attended = outputs.transpose(1, 0, 2).reshape(QROWS, HEADS * HD).astype(jnp.bfloat16)
    mixed = jnp.dot(attended, out_weight, preferred_element_type=jnp.float32)
    return mixed
```

```python
import functools

import jax
import jax.numpy as jnp
from jax import lax
from jax.experimental import pallas as pl
from jax.experimental.pallas import tpu as pltpu
from jax.sharding import PartitionSpec as P

HD = 128
SCALE2 = HD ** (-0.5) * 1.4426950408889634
CHUNK = 512
TAIL = 16
LARGE = 2.0**100
MIB = 1024 * 1024
Z, Y = 8, 4
NT = (((1,), (1,)), ((), ()))
F32 = jnp.float32
BF16 = jnp.bfloat16
VMEM = pl.BlockSpec(memory_space=pltpu.VMEM)
ANY = pl.BlockSpec(memory_space=pl.ANY)
HBM = pl.BlockSpec(memory_space=pltpu.HBM)


def dot(a, b, dims=(((1,), (0,)), ((), ()))):
    return lax.dot_general(a, b, dims, preferred_element_type=F32)


def lse_rows(lse):
    at = lax.broadcasted_iota(jnp.int32, (8, HD), 0)
    row = jnp.broadcast_to(lse, (8, HD))
    hi = row.astype(BF16).astype(F32)
    mid = (row - hi).astype(BF16).astype(F32)
    out = jnp.where(at == 0, hi, jnp.where(at == 1, mid, jnp.where(at == 2, row - hi - mid, 0.0)))
    return jnp.concatenate([out, jnp.zeros((TAIL - 8, HD), F32)], axis=0).astype(BF16)


def lse_of(tail):
    parts = tail[0:3].astype(F32)
    return parts[0:1] + parts[1:2] + parts[2:3]


def attend_kernel(count, *refs):
    q_refs, refs = refs[:count], refs[count:]
    ckt_ref, nkt_ref, cv_ref, nv_ref, more_ref = refs[:5]
    own_refs, oth_ref = refs[5 : 5 + count], refs[5 + count]
    q_s, o_s, lse_s, tot_s = refs[6 + count :]
    pair = q_refs[0].shape[0]
    rows = pair // 2
    groups = cv_ref.shape[1] // HD
    keys = cv_ref.shape[0]
    chunks = [slice(at, at + CHUNK) for at in range(0, keys, CHUNK)]
    for at, ref in enumerate(q_refs):
        q_s[at * pair : (at + 1) * pair] = ref[...]

    def cols_of(h):
        return pl.ds(pl.multiple_of(h * HD, HD), HD)

    def lanes(p):
        return functools.reduce(jnp.add, [p[:, at : at + HD] for at in range(0, p.shape[1], HD)])

    def finish(h, o, shift, total):
        o_s[h] = (o * (1.0 / total)).astype(BF16)
        lse_s[h] = jnp.broadcast_to(shift + jnp.log2(total), lse_s.shape[1:])

    def head(h, _):
        cols = cols_of(h)
        q = q_s[:, cols]
        s_new = dot(q, nkt_ref[cols, :])
        s = dot(q, ckt_ref[cols, chunks[0]])
        shift = jnp.max(s_new, axis=1, keepdims=True) * SCALE2
        p = jnp.exp2(s_new * SCALE2 - shift)
        total = jnp.sum(p, axis=1, keepdims=True)
        o = dot(p.astype(BF16), nv_ref[:, cols])
        wide = 0.0
        for at, chunk in enumerate(chunks):
            if at + 1 < len(chunks):
                s_next = dot(q, ckt_ref[cols, chunks[at + 1]])
            p = jnp.exp2(s * SCALE2 - shift)
            wide += lanes(p)
            o += dot(p.astype(BF16), cv_ref[chunk, cols])
            if at + 1 < len(chunks):
                s = s_next
        total += jnp.sum(wide, axis=1, keepdims=True)
        finish(h, o, shift, total)
        tot_s[h] = jnp.broadcast_to(total, tot_s.shape[1:])
        return 0

    lax.fori_loop(0, groups, head, 0)

    fits = jnp.min(jnp.where(tot_s[...] <= LARGE, 1.0, 0.0))

    @pl.when(fits < 0.5)
    def _():
        def careful(h, _):
            cols = cols_of(h)
            q = q_s[:, cols]
            s_new = dot(q, nkt_ref[cols, :])

            def chunk_at(j):
                return pl.ds(pl.multiple_of(j * HD, HD), HD)

            def peak_of(j, peak):
                s = dot(q, ckt_ref[cols, chunk_at(j)])
                return jnp.maximum(peak, jnp.max(s, axis=1, keepdims=True))

            turns = keys // HD
            peak = lax.fori_loop(0, turns, peak_of, jnp.max(s_new, axis=1, keepdims=True))
            p = jnp.exp2((s_new - peak) * SCALE2)

            def add(j, carried):
                o, total = carried
                p = jnp.exp2((dot(q, ckt_ref[cols, chunk_at(j)]) - peak) * SCALE2)
                o += dot(p.astype(BF16), cv_ref[chunk_at(j), cols])
                return o, total + jnp.sum(p, axis=1, keepdims=True)

            first = (dot(p.astype(BF16), nv_ref[:, cols]), jnp.sum(p, axis=1, keepdims=True))
            o, total = lax.fori_loop(0, turns, add, first)
            finish(h, o, peak * SCALE2, total)
            return 0

        lax.fori_loop(0, groups, careful, 0)

    each = rows + TAIL
    if oth_ref.shape[0] > count * each:
        oth_ref[count * each :] = more_ref[...]
    for h in range(groups):
        cols = slice(h * HD, (h + 1) * HD)
        for at, ref in enumerate(own_refs):
            for side, (to, base) in enumerate(((ref, 0), (oth_ref, at * each))):
                begin = at * pair + side * rows
                to[base : base + rows, cols] = o_s[h, begin : begin + rows]
                lse = lse_s[h, begin : begin + rows]
                lse = jnp.concatenate([lse, jnp.zeros((HD - rows, HD), F32)], axis=0).T
                to[base + rows : base + each, cols] = lse_rows(lse[0:1])


def attend(blocks, ckt, nkt, cv, nv, more=None, after=None):
    count = len(blocks)
    pair, width = blocks[0].shape
    wide = count * pair
    groups = width // HD
    keys = cv.shape[0] + nv.shape[0]
    each = pair // 2 + TAIL
    extra = 0 if more is None else more.shape[0]
    last = (after if more is None else more, ANY if more is None else VMEM)
    return pl.pallas_call(
        functools.partial(attend_kernel, count),
        in_specs=[VMEM] * (count + 4) + [last[1]],
        out_specs=[VMEM] * (count + 1),
        out_shape=[jax.ShapeDtypeStruct((each, width), BF16)] * count
        + [jax.ShapeDtypeStruct((count * each + extra, width), BF16)],
        scratch_shapes=[
            pltpu.VMEM((wide, width), BF16),
            pltpu.VMEM((groups, wide, HD), BF16),
            pltpu.VMEM((groups, wide, HD), F32),
            pltpu.VMEM((groups, wide, HD), F32),
        ],
        compiler_params=pltpu.CompilerParams(vmem_limit_bytes=24 * MIB),
        cost_estimate=pl.CostEstimate(
            flops=12 * wide * keys * width, bytes_accessed=10**6, transcendentals=0
        ),
    )(*blocks, ckt, nkt, cv, nv, last[0])


def merged_heads(blocks):
    rows = blocks[0].shape[0] - TAIL
    groups = blocks[0].shape[1] // HD
    lses = [lse_of(block[rows:]) for block in blocks]
    high = functools.reduce(jnp.maximum, lses)
    weights = [jnp.exp2(lse - high) for lse in lses]
    total = functools.reduce(jnp.add, weights)
    lse = high + jnp.log2(total)
    packed = [weight / total for weight in weights]
    packed = [share[:, h * HD : (h + 1) * HD] for share in packed for h in range(groups)]
    square = jnp.concatenate(packed + [jnp.zeros((HD - len(packed), HD), F32)], axis=0).T
    for h in range(groups):
        cols = slice(h * HD, (h + 1) * HD)
        merged = 0.0
        for at, block in enumerate(blocks):
            column = at * groups + h
            merged += square[:rows, column : column + 1] * block[:rows, cols].astype(F32)
        yield cols, merged, lse[:, cols]


def merge_kernel(*refs):
    out_ref = refs[-1]
    rows = out_ref.shape[0] - TAIL
    for cols, merged, lse in merged_heads([ref[...] for ref in refs[:-1]]):
        out_ref[:rows, cols] = merged.astype(BF16)
        out_ref[rows:, cols] = lse_rows(lse)


def across_kernel(count, *refs):
    mine, theirs_ref, outs = refs[:count], refs[count], refs[count + 1 :]
    each = outs[0].shape[0]
    for at, (mine_ref, out_ref) in enumerate(zip(mine, outs)):
        for cols, merged, lse in merged_heads(
            [mine_ref[...], theirs_ref[at * each : (at + 1) * each]]
        ):
            out_ref[: each - TAIL, cols] = merged.astype(BF16)
            out_ref[each - TAIL :, cols] = lse_rows(lse)


def last_kernel(*refs):
    for cols, merged, _ in merged_heads([ref[...] for ref in refs[:-1]]):
        refs[-1][:, cols] = merged.astype(BF16)


def small(kernel, out_shape, *operands):
    return pl.pallas_call(
        kernel,
        out_shape=out_shape,
        compiler_params=pltpu.CompilerParams(vmem_limit_bytes=6 * MIB),
        cost_estimate=pl.CostEstimate(flops=1, bytes_accessed=1, transcendentals=0),
    )(*operands)


def ready_kernel(q_in, ck_in, nk_in, cv_in, nv_in, q_ref, ckt_ref, nkt_ref, cv_ref, nv_ref, ck_s, nk_s, sems):
    heads = [slice(at, at + HD) for at in range(0, ck_in.shape[1], HD)]
    chunks = [slice(at, at + CHUNK) for at in range(0, ck_in.shape[0], CHUNK)]
    moves = [(ck_in.at[chunk], ck_s.at[chunk]) for chunk in chunks]
    moves += [(nk_in, nk_s), (q_in, q_ref), (nv_in, nv_ref), (cv_in, cv_ref)]
    copies = [pltpu.make_async_copy(a, b, sems.at[at]) for at, (a, b) in enumerate(moves)]
    for copy in copies:
        copy.start()
    for at, chunk in enumerate(chunks):
        copies[at].wait()
        for cols in heads:
            ckt_ref[cols, chunk] = ck_s[chunk, cols].T
    copies[len(chunks)].wait()
    for cols in heads:
        nkt_ref[cols, :] = nk_s[:, cols].T
    for copy in copies[len(chunks) + 1 :]:
        copy.wait()


def ready(q, ck, nk, cv, nv):
    shapes = [q.shape, ck.shape[::-1], nk.shape[::-1], cv.shape, nv.shape]
    return pl.pallas_call(
        ready_kernel,
        in_specs=[HBM] * 5,
        out_specs=[VMEM] * 5,
        out_shape=[jax.ShapeDtypeStruct(shape, BF16) for shape in shapes],
        scratch_shapes=[
            pltpu.VMEM(ck.shape, BF16),
            pltpu.VMEM(nk.shape, BF16),
            pltpu.SemaphoreType.DMA((ck.shape[0] // CHUNK + 4,)),
        ],
        compiler_params=pltpu.CompilerParams(vmem_limit_bytes=12 * MIB),
        cost_estimate=pl.CostEstimate(flops=0, bytes_accessed=7 * 10**6, transcendentals=0),
    )(*[pltpu.with_memory_space_constraint(array, pltpu.HBM) for array in (q, ck, nk, cv, nv)])


def pair_kernel(own_ref, oth_ref, _, out_ref):
    rows = own_ref.shape[0]
    out_ref[:rows] = own_ref[...]
    out_ref[rows:] = oth_ref[...]


def pair(own, oth, after):
    rows, width = own.shape
    return pl.pallas_call(
        pair_kernel,
        in_specs=[VMEM, VMEM, ANY],
        out_specs=VMEM,
        out_shape=jax.ShapeDtypeStruct((2 * rows, width), own.dtype),
        compiler_params=pltpu.CompilerParams(vmem_limit_bytes=4 * MIB),
    )(own, oth, after)


def gate_kernel(*refs):
    del refs


def gate(arrays, after):
    count = len(arrays)
    return pl.pallas_call(
        gate_kernel,
        in_specs=[ANY] * (count + 1),
        out_specs=[ANY] * count,
        out_shape=[jax.ShapeDtypeStruct(array.shape, array.dtype) for array in arrays],
        input_output_aliases={at: at for at in range(count)},
        compiler_params=pltpu.CompilerParams(vmem_limit_bytes=MIB),
    )(*arrays, after)


def arrange_kernel(y_ref, hi_ref, core_ref, own_ref, oth_ref, _, out_ref, sems):
    depth = own_ref.shape[0]
    block = own_ref.shape[1] // 16
    y, x_hi, core = y_ref[0], hi_ref[0], core_ref[0]

    def copy(at, side, ref):
        by, flip = at // 2, at % 2
        x_to = x_hi + flip - 2 * x_hi * flip
        first = (lax.rem(y + by, Y) * 4 + x_to * 2 + core) * block
        return pltpu.make_async_copy(
            ref.at[:, pl.ds(pl.multiple_of(first, HD), block)],
            out_ref.at[pl.ds(side * depth, depth), pl.ds(at * block, block)],
            sems.at[2 * at + side],
        )

    copies = [copy(at, side, ref) for at in range(8) for side, ref in enumerate((own_ref, oth_ref))]
    for one in copies:
        one.start()
    for one in copies:
        one.wait()


def arrange(own, oth, y, x_hi, core, after):
    depth, wide = own.shape
    smem = pl.BlockSpec(memory_space=pltpu.SMEM)
    return pl.pallas_call(
        arrange_kernel,
        in_specs=[smem, smem, smem, ANY, ANY, ANY],
        out_specs=VMEM,
        out_shape=jax.ShapeDtypeStruct((2 * depth, wide // 2), own.dtype),
        scratch_shapes=[pltpu.SemaphoreType.DMA((16,))],
        compiler_params=pltpu.CompilerParams(vmem_limit_bytes=8 * MIB),
        cost_estimate=pl.CostEstimate(flops=0, bytes_accessed=10**7, transcendentals=0),
    )(
        y.reshape(1),
        x_hi.reshape(1),
        core.reshape(1),
        pltpu.with_memory_space_constraint(own, pltpu.HBM),
        oth,
        after,
    )


def share_of(heads, weight_ref, by):
    return dot(heads, weight_ref[:, by * 6 * HD : (by + 1) * 6 * HD])


def both_of(own_ref, oth_ref):
    return jnp.concatenate([own_ref[...], oth_ref[...]], axis=1)


def far_kernel(own_ref, oth_ref, weight_ref, a_ref, b_ref):
    half = a_ref.shape[1]
    share = share_of(both_of(own_ref, oth_ref), weight_ref, 2)
    a_ref[...] = share[:, :half].astype(BF16)
    b_ref[...] = share[:, half:].astype(BF16)


def home_kernel(own_ref, oth_ref, weight_ref, out_ref):
    out_ref[...] = share_of(both_of(own_ref, oth_ref), weight_ref, 0)


def near_kernel(own_ref, oth_ref, weight_ref, a_ref, b_ref, up_ref, down_ref):
    half = a_ref.shape[1]
    heads = both_of(own_ref, oth_ref)
    share = share_of(heads, weight_ref, 1)
    up_ref[:, :half] = (share[:, :half] + a_ref[...].astype(F32)).astype(BF16)
    up_ref[:, half:] = share[:, half:].astype(BF16)
    share = share_of(heads, weight_ref, 3)
    down_ref[:, :half] = share[:, :half].astype(BF16)
    down_ref[:, half:] = (share[:, half:] + b_ref[...].astype(F32)).astype(BF16)


def sum_kernel(home_ref, up_ref, down_ref, own_ref, oth_ref):
    half = own_ref.shape[1]
    total = home_ref[...] + up_ref[...].astype(F32) + down_ref[...].astype(F32)
    own_ref[...] = total[:, :half]
    oth_ref[...] = total[:, half:].astype(BF16)


def projecting(kernel, out_shape, *operands):
    rows, depth = operands[0].shape
    return pl.pallas_call(
        kernel,
        out_shape=out_shape,
        compiler_params=pltpu.CompilerParams(vmem_limit_bytes=14 * MIB),
        cost_estimate=pl.CostEstimate(
            flops=16 * rows * depth * depth, bytes_accessed=2 * 10**6, transcendentals=0
        ),
    )(*operands)


def body(queries, new_keys, new_values, cache_keys, cache_values, out_weight):
    rows, width = queries.shape
    head_at = lax.axis_index("head").astype(jnp.int32)
    core, x_hi, y = head_at & 1, (head_at >> 1) & 1, head_at >> 2

    def along_z(array, by):
        return lax.ppermute(
            array, "ctx", [(x * Z + z, x * Z + (z + by) % Z) for x in range(2) for z in range(Z)]
        )

    def across_x(array):
        return lax.ppermute(array, "ctx", [(i, (i + Z) % (2 * Z)) for i in range(2 * Z)])

    def across_core(array):
        return lax.ppermute(array, "head", [(i, i ^ 1) for i in range(4 * Y)])

    def across_hi(array):
        return lax.ppermute(array, "head", [(i, i ^ 2) for i in range(4 * Y)])

    def along_y(array, by):
        return lax.ppermute(array, "head", [(i, (i + 4 * by) % (4 * Y)) for i in range(4 * Y)])

    def shape(*dims, dtype=BF16):
        return jax.ShapeDtypeStruct(dims, dtype)

    weight_oth = across_core(out_weight)
    q_here, *cached = ready(queries, cache_keys, new_keys, cache_values, new_values)
    q = {0: pair(q_here, across_x(queries), cached[0])}
    q[1], q[-1] = along_z(q[0], -1), along_z(q[0], 1)
    part = {}
    part[0], oth = attend([q[0]], *cached, after=q_here)
    ahead = [along_z(q[1], -1), along_z(q[-1], 1)]
    part[1], part[-1], oth = attend([q[1], q[-1]], *cached, more=oth)
    q[2], q[-2] = gate(ahead, part[1])
    ahead = [along_z(q[2], -1), along_z(q[-2], 1)]
    part[2], part[-2], near = attend([q[2], q[-2]], *cached, more=oth)
    q[3], q[-3] = gate(ahead, part[2])
    ahead = along_z(q[3], -1)
    part[3], part[-3], far = attend([q[3], q[-3]], *cached, after=part[2])
    (q[4],) = gate([ahead], part[3])
    part[4], last = attend([q[4]], *cached, after=part[3])

    one = shape(rows + TAIL, width)

    def merged(theirs, *blocks):
        out = small(
            functools.partial(across_kernel, len(blocks)),
            [one] * len(blocks),
            *[part[d] for d in blocks],
            theirs,
        )
        part.update(zip(blocks, out))

    near = across_x(gate([near], q[3])[0])
    far = across_x(gate([far], q[4])[0])
    weight = arrange(out_weight, weight_oth, y, x_hi, core, part[4])
    last = gate([across_x(last)], weight)[0]
    merged(far, 3, -3)
    merged(near, 2, -2, 1, -1, 0)
    merged(last, 4)
    back = [along_z(part[d], d) for d in (4, 3, -3, 2, -2, 1, -1)]
    own = small(last_kernel, shape(rows, width), part[0], *back)

    oth = across_core(own)
    a, b = projecting(far_kernel, [shape(rows, width)] * 2, own, oth, weight)
    a, b = along_y(a, 1), along_y(b, -1)
    home = projecting(home_kernel, shape(rows, 2 * width, dtype=F32), own, oth, weight)
    up, down = projecting(near_kernel, [shape(rows, 2 * width)] * 2, own, oth, weight, a, b)
    ours, rest = small(
        sum_kernel,
        [shape(rows, width, dtype=F32), shape(rows, width)],
        home,
        along_y(up, 1),
        along_y(down, -1),
    )
    return ours + across_hi(rest).astype(F32)


def solution(mesh):
    placed = (
        P("ctx", "head"),
        P("ctx", "head"),
        P("ctx", "head"),
        P("ctx", "head"),
        P("ctx", "head"),
        P("head", None),
    )
    return jax.shard_map(
        body, mesh=mesh, in_specs=placed, out_specs=P("ctx", "head"), check_vma=False
    )
```

```python
import functools

import jax
import jax.numpy as jnp
from jax import lax
from jax.experimental import pallas as pl
from jax.experimental.pallas import tpu as pltpu
from jax.sharding import PartitionSpec as P

HD = 128
SCALE2 = HD ** (-0.5) * 1.4426950408889634
CHUNK = 512
TAIL = 16
LARGE = 2.0**100
MIB = 1024 * 1024
Z, Y = 8, 4
NT = (((1,), (1,)), ((), ()))
F32 = jnp.float32
BF16 = jnp.bfloat16
VMEM = pl.BlockSpec(memory_space=pltpu.VMEM)
ANY = pl.BlockSpec(memory_space=pl.ANY)
HBM = pl.BlockSpec(memory_space=pltpu.HBM)


def dot(a, b, dims=(((1,), (0,)), ((), ()))):
    return lax.dot_general(a, b, dims, preferred_element_type=F32)


def lse_rows(lse):
    at = lax.broadcasted_iota(jnp.int32, (8, HD), 0)
    row = jnp.broadcast_to(lse, (8, HD))
    hi = row.astype(BF16).astype(F32)
    mid = (row - hi).astype(BF16).astype(F32)
    out = jnp.where(at == 0, hi, jnp.where(at == 1, mid, jnp.where(at == 2, row - hi - mid, 0.0)))
    return jnp.concatenate([out, jnp.zeros((TAIL - 8, HD), F32)], axis=0).astype(BF16)


def lse_of(tail):
    parts = tail[0:3].astype(F32)
    return parts[0:1] + parts[1:2] + parts[2:3]


def attend_kernel(count, *refs):
    q_refs, refs = refs[:count], refs[count:]
    ck_ref, nk_ref, cvt_ref, nvt_ref, more_ref = refs[:5]
    own_refs, oth_ref = refs[5 : 5 + count], refs[5 + count]
    q_s, ot_s, lse_s, tot_s = refs[6 + count :]
    pair = q_refs[0].shape[0]
    rows = pair // 2
    wide = q_s.shape[0]
    groups = ck_ref.shape[1] // HD
    chunks = ck_ref.shape[0] // CHUNK
    for at, ref in enumerate(q_refs):
        q_s[at * pair : (at + 1) * pair] = ref[...]
    if wide > count * pair:
        q_s[count * pair :] = jnp.zeros((wide - count * pair, q_s.shape[1]), BF16)

    def cols_of(h):
        return pl.ds(pl.multiple_of(h * HD, HD), HD)

    def head(h, _):
        cols = cols_of(h)
        q = q_s[:, cols]
        s_new = dot(nk_ref[:, cols], q, NT)
        s = dot(ck_ref[0:CHUNK, cols], q, NT)
        shift = jnp.max(s_new, axis=0, keepdims=True) * SCALE2
        p = jnp.exp2(s_new * SCALE2 - shift)
        total = jnp.sum(p, axis=0, keepdims=True)
        o = dot(nvt_ref[cols, :], p.astype(BF16))
        for j in range(chunks):
            if j + 1 < chunks:
                s_next = dot(ck_ref[(j + 1) * CHUNK : (j + 2) * CHUNK, cols], q, NT)
            p = jnp.exp2(s * SCALE2 - shift)
            total += jnp.sum(p, axis=0, keepdims=True)
            o += dot(cvt_ref[cols, j * CHUNK : (j + 1) * CHUNK], p.astype(BF16))
            if j + 1 < chunks:
                s = s_next
        ot_s[h] = o * (1.0 / total)
        lse_s[h] = jnp.broadcast_to(shift + jnp.log2(total), (8, wide))
        tot_s[h] = jnp.broadcast_to(total, (8, wide))
        return 0

    lax.fori_loop(0, groups, head, 0)

    fits = jnp.min(jnp.where(tot_s[...] <= LARGE, 1.0, 0.0))

    @pl.when(fits < 0.5)
    def _():
        def careful(h, _):
            cols = cols_of(h)
            q = q_s[:, cols]
            s_new = dot(nk_ref[:, cols], q, NT)

            def chunk_at(j):
                return pl.ds(pl.multiple_of(j * HD, HD), HD)

            def peak_of(j, peak):
                s = dot(ck_ref[chunk_at(j), cols], q, NT)
                return jnp.maximum(peak, jnp.max(s, axis=0, keepdims=True))

            turns = ck_ref.shape[0] // HD
            peak = lax.fori_loop(0, turns, peak_of, jnp.max(s_new, axis=0, keepdims=True))
            p = jnp.exp2((s_new - peak) * SCALE2)
            ot_s[h] = dot(nvt_ref[cols, :], p.astype(BF16))

            def add(j, total):
                s = dot(ck_ref[chunk_at(j), cols], q, NT)
                p = jnp.exp2((s - peak) * SCALE2)
                ot_s[h] += dot(cvt_ref[cols, chunk_at(j)], p.astype(BF16))
                return total + jnp.sum(p, axis=0, keepdims=True)

            total = lax.fori_loop(0, turns, add, jnp.sum(p, axis=0, keepdims=True))
            ot_s[h] = ot_s[h] * (1.0 / total)
            lse_s[h] = jnp.broadcast_to(peak * SCALE2 + jnp.log2(total), (8, wide))
            return 0

        lax.fori_loop(0, groups, careful, 0)

    each = rows + TAIL
    if oth_ref.shape[0] > count * each:
        oth_ref[count * each :] = more_ref[...]
    for h in range(groups):
        cols = slice(h * HD, (h + 1) * HD)
        o = ot_s[h].T.astype(BF16)
        lse = lse_s[h]
        for at, ref in enumerate(own_refs):
            for side, (to, base) in enumerate(((ref, 0), (oth_ref, at * each))):
                begin = at * pair + side * rows
                to[base : base + rows, cols] = o[begin : begin + rows]
                turned = pltpu.roll(lse, wide - begin, axis=1) if begin else lse
                to[base + rows : base + each, cols] = lse_rows(turned[0:1, :HD])


def attend(blocks, ck, nk, cvt, nvt, more=None, after=None):
    count = len(blocks)
    pair, width = blocks[0].shape
    wide = -(-count * pair // HD) * HD
    groups = width // HD
    keys = ck.shape[0] + nk.shape[0]
    each = pair // 2 + TAIL
    extra = 0 if more is None else more.shape[0]
    last = (after if more is None else more, ANY if more is None else VMEM)
    return pl.pallas_call(
        functools.partial(attend_kernel, count),
        in_specs=[VMEM] * (count + 4) + [last[1]],
        out_specs=[VMEM] * (count + 1),
        out_shape=[jax.ShapeDtypeStruct((each, width), BF16)] * count
        + [jax.ShapeDtypeStruct((count * each + extra, width), BF16)],
        scratch_shapes=[
            pltpu.VMEM((wide, width), BF16),
            pltpu.VMEM((groups, HD, wide), F32),
            pltpu.VMEM((groups, 8, wide), F32),
            pltpu.VMEM((groups, 8, wide), F32),
        ],
        compiler_params=pltpu.CompilerParams(vmem_limit_bytes=24 * MIB),
        cost_estimate=pl.CostEstimate(
            flops=12 * wide * keys * width, bytes_accessed=10**6, transcendentals=0
        ),
    )(*blocks, ck, nk, cvt, nvt, last[0])


def merged_heads(blocks):
    rows = blocks[0].shape[0] - TAIL
    groups = blocks[0].shape[1] // HD
    lses = [lse_of(block[rows:]) for block in blocks]
    high = functools.reduce(jnp.maximum, lses)
    weights = [jnp.exp2(lse - high) for lse in lses]
    total = functools.reduce(jnp.add, weights)
    lse = high + jnp.log2(total)
    packed = [weight / total for weight in weights]
    packed = [share[:, h * HD : (h + 1) * HD] for share in packed for h in range(groups)]
    square = jnp.concatenate(packed + [jnp.zeros((HD - len(packed), HD), F32)], axis=0).T
    for h in range(groups):
        cols = slice(h * HD, (h + 1) * HD)
        merged = 0.0
        for at, block in enumerate(blocks):
            column = at * groups + h
            merged += square[:rows, column : column + 1] * block[:rows, cols].astype(F32)
        yield cols, merged, lse[:, cols]


def merge_kernel(*refs):
    out_ref = refs[-1]
    rows = out_ref.shape[0] - TAIL
    for cols, merged, lse in merged_heads([ref[...] for ref in refs[:-1]]):
        out_ref[:rows, cols] = merged.astype(BF16)
        out_ref[rows:, cols] = lse_rows(lse)


def across_kernel(count, *refs):
    mine, theirs_ref, outs = refs[:count], refs[count], refs[count + 1 :]
    each = outs[0].shape[0]
    for at, (mine_ref, out_ref) in enumerate(zip(mine, outs)):
        for cols, merged, lse in merged_heads(
            [mine_ref[...], theirs_ref[at * each : (at + 1) * each]]
        ):
            out_ref[: each - TAIL, cols] = merged.astype(BF16)
            out_ref[each - TAIL :, cols] = lse_rows(lse)


def last_kernel(*refs):
    for cols, merged, _ in merged_heads([ref[...] for ref in refs[:-1]]):
        refs[-1][:, cols] = merged.astype(BF16)


def small(kernel, out_shape, *operands):
    return pl.pallas_call(
        kernel,
        out_shape=out_shape,
        compiler_params=pltpu.CompilerParams(vmem_limit_bytes=6 * MIB),
        cost_estimate=pl.CostEstimate(flops=1, bytes_accessed=1, transcendentals=0),
    )(*operands)


def ready_kernel(q_in, ck_in, nk_in, cv_in, nv_in, q_ref, ck_ref, nk_ref, cvt_ref, nvt_ref, cv_s, nv_s, sems):
    chunks = cv_in.shape[0] // CHUNK
    parts = [pl.ds(at * CHUNK, CHUNK) for at in range(chunks)]
    moves = [(cv_in.at[part], cv_s.at[part]) for part in parts]
    moves += [(nv_in, nv_s), (ck_in, ck_ref), (nk_in, nk_ref), (q_in, q_ref)]
    copies = [pltpu.make_async_copy(a, b, sems.at[at]) for at, (a, b) in enumerate(moves)]
    for copy in copies:
        copy.start()
    for at in range(chunks):
        copies[at].wait()
        for h in range(cv_in.shape[1] // HD):
            cols = slice(h * HD, (h + 1) * HD)
            cvt_ref[cols, at * CHUNK : (at + 1) * CHUNK] = cv_s[at * CHUNK : (at + 1) * CHUNK, cols].T
    copies[chunks].wait()
    for h in range(cv_in.shape[1] // HD):
        cols = slice(h * HD, (h + 1) * HD)
        nvt_ref[cols, :] = nv_s[:, cols].T
    for copy in copies[chunks + 1 :]:
        copy.wait()


def ready(q, ck, nk, cv, nv):
    shapes = [q.shape, ck.shape, nk.shape, cv.shape[::-1], nv.shape[::-1]]
    return pl.pallas_call(
        ready_kernel,
        in_specs=[HBM] * 5,
        out_specs=[VMEM] * 5,
        out_shape=[jax.ShapeDtypeStruct(shape, BF16) for shape in shapes],
        scratch_shapes=[
            pltpu.VMEM(cv.shape, BF16),
            pltpu.VMEM(nv.shape, BF16),
            pltpu.SemaphoreType.DMA((cv.shape[0] // CHUNK + 4,)),
        ],
        compiler_params=pltpu.CompilerParams(vmem_limit_bytes=12 * MIB),
        cost_estimate=pl.CostEstimate(flops=0, bytes_accessed=7 * 10**6, transcendentals=0),
    )(*[pltpu.with_memory_space_constraint(array, pltpu.HBM) for array in (q, ck, nk, cv, nv)])


def pair_kernel(own_ref, oth_ref, _, out_ref):
    rows = own_ref.shape[0]
    out_ref[:rows] = own_ref[...]
    out_ref[rows:] = oth_ref[...]


def pair(own, oth, after):
    rows, width = own.shape
    return pl.pallas_call(
        pair_kernel,
        in_specs=[VMEM, VMEM, ANY],
        out_specs=VMEM,
        out_shape=jax.ShapeDtypeStruct((2 * rows, width), own.dtype),
        compiler_params=pltpu.CompilerParams(vmem_limit_bytes=4 * MIB),
    )(own, oth, after)


def gate_kernel(*refs):
    del refs


def gate(arrays, after):
    count = len(arrays)
    return pl.pallas_call(
        gate_kernel,
        in_specs=[ANY] * (count + 1),
        out_specs=[ANY] * count,
        out_shape=[jax.ShapeDtypeStruct(array.shape, array.dtype) for array in arrays],
        input_output_aliases={at: at for at in range(count)},
        compiler_params=pltpu.CompilerParams(vmem_limit_bytes=MIB),
    )(*arrays, after)


def arrange_kernel(y_ref, hi_ref, core_ref, own_ref, oth_ref, _, out_ref, sems):
    depth = own_ref.shape[0]
    block = own_ref.shape[1] // 16
    y, x_hi, core = y_ref[0], hi_ref[0], core_ref[0]

    def copy(at, side, ref):
        by, flip = at // 2, at % 2
        x_to = x_hi + flip - 2 * x_hi * flip
        first = (lax.rem(y + by, Y) * 4 + x_to * 2 + core) * block
        return pltpu.make_async_copy(
            ref.at[:, pl.ds(pl.multiple_of(first, HD), block)],
            out_ref.at[pl.ds(side * depth, depth), pl.ds(at * block, block)],
            sems.at[2 * at + side],
        )

    copies = [copy(at, side, ref) for at in range(8) for side, ref in enumerate((own_ref, oth_ref))]
    for one in copies:
        one.start()
    for one in copies:
        one.wait()


def arrange(own, oth, y, x_hi, core, after):
    depth, wide = own.shape
    smem = pl.BlockSpec(memory_space=pltpu.SMEM)
    return pl.pallas_call(
        arrange_kernel,
        in_specs=[smem, smem, smem, ANY, ANY, ANY],
        out_specs=VMEM,
        out_shape=jax.ShapeDtypeStruct((2 * depth, wide // 2), own.dtype),
        scratch_shapes=[pltpu.SemaphoreType.DMA((16,))],
        compiler_params=pltpu.CompilerParams(vmem_limit_bytes=8 * MIB),
        cost_estimate=pl.CostEstimate(flops=0, bytes_accessed=10**7, transcendentals=0),
    )(
        y.reshape(1),
        x_hi.reshape(1),
        core.reshape(1),
        pltpu.with_memory_space_constraint(own, pltpu.HBM),
        oth,
        after,
    )


def share_of(heads, weight_ref, by):
    return dot(heads, weight_ref[:, by * 6 * HD : (by + 1) * 6 * HD])


def both_of(own_ref, oth_ref):
    return jnp.concatenate([own_ref[...], oth_ref[...]], axis=1)


def far_kernel(own_ref, oth_ref, weight_ref, a_ref, b_ref):
    half = a_ref.shape[1]
    share = share_of(both_of(own_ref, oth_ref), weight_ref, 2)
    a_ref[...] = share[:, :half].astype(BF16)
    b_ref[...] = share[:, half:].astype(BF16)


def home_kernel(own_ref, oth_ref, weight_ref, out_ref):
    out_ref[...] = share_of(both_of(own_ref, oth_ref), weight_ref, 0)


def near_kernel(own_ref, oth_ref, weight_ref, a_ref, b_ref, up_ref, down_ref):
    half = a_ref.shape[1]
    heads = both_of(own_ref, oth_ref)
    share = share_of(heads, weight_ref, 1)
    up_ref[:, :half] = (share[:, :half] + a_ref[...].astype(F32)).astype(BF16)
    up_ref[:, half:] = share[:, half:].astype(BF16)
    share = share_of(heads, weight_ref, 3)
    down_ref[:, :half] = share[:, :half].astype(BF16)
    down_ref[:, half:] = (share[:, half:] + b_ref[...].astype(F32)).astype(BF16)


def sum_kernel(home_ref, up_ref, down_ref, own_ref, oth_ref):
    half = own_ref.shape[1]
    total = home_ref[...] + up_ref[...].astype(F32) + down_ref[...].astype(F32)
    own_ref[...] = total[:, :half]
    oth_ref[...] = total[:, half:].astype(BF16)


def projecting(kernel, out_shape, *operands):
    rows, depth = operands[0].shape
    return pl.pallas_call(
        kernel,
        out_shape=out_shape,
        compiler_params=pltpu.CompilerParams(vmem_limit_bytes=14 * MIB),
        cost_estimate=pl.CostEstimate(
            flops=16 * rows * depth * depth, bytes_accessed=2 * 10**6, transcendentals=0
        ),
    )(*operands)


def body(queries, new_keys, new_values, cache_keys, cache_values, out_weight):
    rows, width = queries.shape
    head_at = lax.axis_index("head").astype(jnp.int32)
    core, x_hi, y = head_at & 1, (head_at >> 1) & 1, head_at >> 2

    def along_z(array, by):
        return lax.ppermute(
            array, "ctx", [(x * Z + z, x * Z + (z + by) % Z) for x in range(2) for z in range(Z)]
        )

    def across_x(array):
        return lax.ppermute(array, "ctx", [(i, (i + Z) % (2 * Z)) for i in range(2 * Z)])

    def across_core(array):
        return lax.ppermute(array, "head", [(i, i ^ 1) for i in range(4 * Y)])

    def across_hi(array):
        return lax.ppermute(array, "head", [(i, i ^ 2) for i in range(4 * Y)])

    def along_y(array, by):
        return lax.ppermute(array, "head", [(i, (i + 4 * by) % (4 * Y)) for i in range(4 * Y)])

    def shape(*dims, dtype=BF16):
        return jax.ShapeDtypeStruct(dims, dtype)

    weight_oth = across_core(out_weight)
    q_here, *cached = ready(queries, cache_keys, new_keys, cache_values, new_values)
    q = {0: pair(q_here, across_x(queries), cached[0])}
    q[1], q[-1] = along_z(q[0], -1), along_z(q[0], 1)
    part = {}
    part[0], oth = attend([q[0]], *cached, after=q_here)
    ahead = [along_z(q[1], -1), along_z(q[-1], 1)]
    part[1], part[-1], oth = attend([q[1], q[-1]], *cached, more=oth)
    q[2], q[-2] = gate(ahead, part[1])
    ahead = [along_z(q[2], -1), along_z(q[-2], 1)]
    part[2], part[-2], near = attend([q[2], q[-2]], *cached, after=part[1])
    q[3], q[-3] = gate(ahead, part[2])
    ahead = along_z(q[3], -1)
    part[3], part[-3], far = attend([q[3], q[-3]], *cached, after=part[2])
    (q[4],) = gate([ahead], part[3])
    part[4], last = attend([q[4]], *cached, after=part[3])

    one = shape(rows + TAIL, width)

    def merged(theirs, *blocks):
        out = small(
            functools.partial(across_kernel, len(blocks)),
            [one] * len(blocks),
            *[part[d] for d in blocks],
            theirs,
        )
        part.update(zip(blocks, out))

    def met(there, here):
        return small(merge_kernel, one, there, here)

    oth = across_x(gate([oth], q[2])[0])
    near = across_x(gate([near], q[3])[0])
    far = across_x(gate([far], q[4])[0])
    weight = arrange(out_weight, weight_oth, y, x_hi, core, last)
    merged(gate([across_x(last)], weight)[0], 4)
    merged(gate([far], part[4])[0], 3, -3)
    merged(gate([near], part[3])[0], 2, -2)
    merged(gate([oth], part[2])[0], 1, -1, 0)
    up = met(along_z(part[4], 1), part[3])
    down = met(gate([along_z(part[-3], -1)], up)[0], part[-2])
    close = met(gate([along_z(part[2], 1)], down)[0], part[1])
    back = [along_z(part[-1], -1), along_z(close, 1), along_z(down, -2), along_z(up, 3)]
    own = small(last_kernel, shape(rows, width), part[0], *back)

    oth = across_core(own)
    a, b = projecting(far_kernel, [shape(rows, width)] * 2, own, oth, weight)
    a, b = along_y(a, 1), along_y(b, -1)
    home = projecting(home_kernel, shape(rows, 2 * width, dtype=F32), own, oth, weight)
    up, down = projecting(near_kernel, [shape(rows, 2 * width)] * 2, own, oth, weight, a, b)
    ours, rest = small(
        sum_kernel,
        [shape(rows, width, dtype=F32), shape(rows, width)],
        home,
        along_y(up, 1),
        along_y(down, -1),
    )
    return ours + across_hi(rest).astype(F32)


def solution(mesh):
    placed = (
        P("ctx", "head"),
        P("ctx", "head"),
        P("ctx", "head"),
        P("ctx", "head"),
        P("ctx", "head"),
        P("head", None),
    )
    return jax.shard_map(
        body, mesh=mesh, in_specs=placed, out_specs=P("ctx", "head"), check_vma=False
    )
```

```python
import functools

import jax
import jax.numpy as jnp
from jax import lax
from jax.experimental import pallas as pl
from jax.experimental.pallas import tpu as pltpu
from jax.sharding import PartitionSpec as P

HD = 128
SCALE2 = HD ** (-0.5) * 1.4426950408889634
CHUNK = 512
TAIL = 16
LARGE = 2.0**100
MIB = 1024 * 1024
Z, Y = 8, 4
NT = (((1,), (1,)), ((), ()))
F32 = jnp.float32
BF16 = jnp.bfloat16
VMEM = pl.BlockSpec(memory_space=pltpu.VMEM)
ANY = pl.BlockSpec(memory_space=pl.ANY)
HBM = pl.BlockSpec(memory_space=pltpu.HBM)


def dot(a, b, dims=(((1,), (0,)), ((), ()))):
    return lax.dot_general(a, b, dims, preferred_element_type=F32)


def lse_rows(lse):
    at = lax.broadcasted_iota(jnp.int32, (8, HD), 0)
    row = jnp.broadcast_to(lse, (8, HD))
    hi = row.astype(BF16).astype(F32)
    mid = (row - hi).astype(BF16).astype(F32)
    out = jnp.where(at == 0, hi, jnp.where(at == 1, mid, jnp.where(at == 2, row - hi - mid, 0.0)))
    return jnp.concatenate([out, jnp.zeros((TAIL - 8, HD), F32)], axis=0).astype(BF16)


def lse_of(tail):
    parts = tail[0:3].astype(F32)
    return parts[0:1] + parts[1:2] + parts[2:3]


def attend_kernel(count, *refs):
    q_refs, refs = refs[:count], refs[count:]
    ck_ref, nk_ref, cvt_ref, nvt_ref, more_ref = refs[:5]
    own_refs, oth_ref = refs[5 : 5 + count], refs[5 + count]
    q_s, ot_s, lse_s, tot_s = refs[6 + count :]
    pair = q_refs[0].shape[0]
    rows = pair // 2
    wide = q_s.shape[0]
    groups = ck_ref.shape[1] // HD
    chunks = ck_ref.shape[0] // CHUNK
    for at, ref in enumerate(q_refs):
        q_s[at * pair : (at + 1) * pair] = ref[...]
    if wide > count * pair:
        q_s[count * pair :] = jnp.zeros((wide - count * pair, q_s.shape[1]), BF16)

    def cols_of(h):
        return pl.ds(pl.multiple_of(h * HD, HD), HD)

    steps = [(h, at) for h in range(groups) for at in range(-1, chunks)]

    def scores(h, at):
        cols = slice(h * HD, (h + 1) * HD)
        keys = nk_ref[:, cols] if at < 0 else ck_ref[at * CHUNK : (at + 1) * CHUNK, cols]
        return dot(keys, q_s[:, cols], NT)

    ahead = scores(*steps[0])
    for index, (h, at) in enumerate(steps):
        s = ahead
        if index + 1 < len(steps):
            ahead = scores(*steps[index + 1])
        cols = slice(h * HD, (h + 1) * HD)
        if at < 0:
            shift = jnp.max(s, axis=0, keepdims=True) * SCALE2
        p = jnp.exp2(s * SCALE2 - shift)
        values = nvt_ref[cols, :] if at < 0 else cvt_ref[cols, at * CHUNK : (at + 1) * CHUNK]
        more = dot(values, p.astype(BF16))
        total = jnp.sum(p, axis=0, keepdims=True) + (0.0 if at < 0 else total)
        o = more if at < 0 else o + more
        if at == chunks - 1:
            ot_s[h] = o * (1.0 / total)
            lse_s[h] = jnp.broadcast_to(shift + jnp.log2(total), (8, wide))
            tot_s[h] = jnp.broadcast_to(total, (8, wide))

    fits = jnp.min(jnp.where(tot_s[...] <= LARGE, 1.0, 0.0))

    @pl.when(fits < 0.5)
    def _():
        def careful(h, _):
            cols = cols_of(h)
            q = q_s[:, cols]
            s_new = dot(nk_ref[:, cols], q, NT)

            def chunk_at(j):
                return pl.ds(pl.multiple_of(j * HD, HD), HD)

            def peak_of(j, peak):
                s = dot(ck_ref[chunk_at(j), cols], q, NT)
                return jnp.maximum(peak, jnp.max(s, axis=0, keepdims=True))

            turns = ck_ref.shape[0] // HD
            peak = lax.fori_loop(0, turns, peak_of, jnp.max(s_new, axis=0, keepdims=True))
            p = jnp.exp2((s_new - peak) * SCALE2)
            ot_s[h] = dot(nvt_ref[cols, :], p.astype(BF16))

            def add(j, total):
                s = dot(ck_ref[chunk_at(j), cols], q, NT)
                p = jnp.exp2((s - peak) * SCALE2)
                ot_s[h] += dot(cvt_ref[cols, chunk_at(j)], p.astype(BF16))
                return total + jnp.sum(p, axis=0, keepdims=True)

            total = lax.fori_loop(0, turns, add, jnp.sum(p, axis=0, keepdims=True))
            ot_s[h] = ot_s[h] * (1.0 / total)
            lse_s[h] = jnp.broadcast_to(peak * SCALE2 + jnp.log2(total), (8, wide))
            return 0

        lax.fori_loop(0, groups, careful, 0)

    each = rows + TAIL
    if oth_ref.shape[0] > count * each:
        oth_ref[count * each :] = more_ref[...]
    for h in range(groups):
        cols = slice(h * HD, (h + 1) * HD)
        o = ot_s[h].T.astype(BF16)
        lse = lse_s[h]
        for at, ref in enumerate(own_refs):
            for side, (to, base) in enumerate(((ref, 0), (oth_ref, at * each))):
                begin = at * pair + side * rows
                to[base : base + rows, cols] = o[begin : begin + rows]
                turned = pltpu.roll(lse, wide - begin, axis=1) if begin else lse
                to[base + rows : base + each, cols] = lse_rows(turned[0:1, :HD])


def attend(blocks, ck, nk, cvt, nvt, more=None, after=None):
    count = len(blocks)
    pair, width = blocks[0].shape
    wide = -(-count * pair // HD) * HD
    groups = width // HD
    keys = ck.shape[0] + nk.shape[0]
    each = pair // 2 + TAIL
    extra = 0 if more is None else more.shape[0]
    last = (after if more is None else more, ANY if more is None else VMEM)
    return pl.pallas_call(
        functools.partial(attend_kernel, count),
        in_specs=[VMEM] * (count + 4) + [last[1]],
        out_specs=[VMEM] * (count + 1),
        out_shape=[jax.ShapeDtypeStruct((each, width), BF16)] * count
        + [jax.ShapeDtypeStruct((count * each + extra, width), BF16)],
        scratch_shapes=[
            pltpu.VMEM((wide, width), BF16),
            pltpu.VMEM((groups, HD, wide), F32),
            pltpu.VMEM((groups, 8, wide), F32),
            pltpu.VMEM((groups, 8, wide), F32),
        ],
        compiler_params=pltpu.CompilerParams(vmem_limit_bytes=24 * MIB),
        cost_estimate=pl.CostEstimate(
            flops=12 * wide * keys * width, bytes_accessed=10**6, transcendentals=0
        ),
    )(*blocks, ck, nk, cvt, nvt, last[0])


def merged_heads(blocks):
    rows = blocks[0].shape[0] - TAIL
    groups = blocks[0].shape[1] // HD
    lses = [lse_of(block[rows:]) for block in blocks]
    high = functools.reduce(jnp.maximum, lses)
    weights = [jnp.exp2(lse - high) for lse in lses]
    total = functools.reduce(jnp.add, weights)
    lse = high + jnp.log2(total)
    packed = [weight / total for weight in weights]
    packed = [share[:, h * HD : (h + 1) * HD] for share in packed for h in range(groups)]
    square = jnp.concatenate(packed + [jnp.zeros((HD - len(packed), HD), F32)], axis=0).T
    for h in range(groups):
        cols = slice(h * HD, (h + 1) * HD)
        merged = 0.0
        for at, block in enumerate(blocks):
            column = at * groups + h
            merged += square[:rows, column : column + 1] * block[:rows, cols].astype(F32)
        yield cols, merged, lse[:, cols]


def merge_kernel(*refs):
    out_ref = refs[-1]
    rows = out_ref.shape[0] - TAIL
    for cols, merged, lse in merged_heads([ref[...] for ref in refs[:-1]]):
        out_ref[:rows, cols] = merged.astype(BF16)
        out_ref[rows:, cols] = lse_rows(lse)


def across_kernel(count, *refs):
    mine, theirs_ref, outs = refs[:count], refs[count], refs[count + 1 :]
    each = outs[0].shape[0]
    for at, (mine_ref, out_ref) in enumerate(zip(mine, outs)):
        for cols, merged, lse in merged_heads(
            [mine_ref[...], theirs_ref[at * each : (at + 1) * each]]
        ):
            out_ref[: each - TAIL, cols] = merged.astype(BF16)
            out_ref[each - TAIL :, cols] = lse_rows(lse)


def last_kernel(*refs):
    for cols, merged, _ in merged_heads([ref[...] for ref in refs[:-1]]):
        refs[-1][:, cols] = merged.astype(BF16)


def small(kernel, out_shape, *operands):
    return pl.pallas_call(
        kernel,
        out_shape=out_shape,
        compiler_params=pltpu.CompilerParams(vmem_limit_bytes=6 * MIB),
        cost_estimate=pl.CostEstimate(flops=1, bytes_accessed=1, transcendentals=0),
    )(*operands)


def ready_kernel(q_in, ck_in, nk_in, cv_in, nv_in, q_ref, ck_ref, nk_ref, cvt_ref, nvt_ref, cv_s, nv_s, sems):
    chunks = cv_in.shape[0] // CHUNK
    parts = [pl.ds(at * CHUNK, CHUNK) for at in range(chunks)]
    moves = [(cv_in.at[part], cv_s.at[part]) for part in parts]
    moves += [(nv_in, nv_s), (ck_in, ck_ref), (nk_in, nk_ref), (q_in, q_ref)]
    copies = [pltpu.make_async_copy(a, b, sems.at[at]) for at, (a, b) in enumerate(moves)]
    for copy in copies:
        copy.start()
    for at in range(chunks):
        copies[at].wait()
        for h in range(cv_in.shape[1] // HD):
            cols = slice(h * HD, (h + 1) * HD)
            cvt_ref[cols, at * CHUNK : (at + 1) * CHUNK] = cv_s[at * CHUNK : (at + 1) * CHUNK, cols].T
    copies[chunks].wait()
    for h in range(cv_in.shape[1] // HD):
        cols = slice(h * HD, (h + 1) * HD)
        nvt_ref[cols, :] = nv_s[:, cols].T
    for copy in copies[chunks + 1 :]:
        copy.wait()


def ready(q, ck, nk, cv, nv):
    shapes = [q.shape, ck.shape, nk.shape, cv.shape[::-1], nv.shape[::-1]]
    return pl.pallas_call(
        ready_kernel,
        in_specs=[HBM] * 5,
        out_specs=[VMEM] * 5,
        out_shape=[jax.ShapeDtypeStruct(shape, BF16) for shape in shapes],
        scratch_shapes=[
            pltpu.VMEM(cv.shape, BF16),
            pltpu.VMEM(nv.shape, BF16),
            pltpu.SemaphoreType.DMA((cv.shape[0] // CHUNK + 4,)),
        ],
        compiler_params=pltpu.CompilerParams(vmem_limit_bytes=12 * MIB),
        cost_estimate=pl.CostEstimate(flops=0, bytes_accessed=7 * 10**6, transcendentals=0),
    )(*[pltpu.with_memory_space_constraint(array, pltpu.HBM) for array in (q, ck, nk, cv, nv)])


def pair_kernel(own_ref, oth_ref, _, out_ref):
    rows = own_ref.shape[0]
    out_ref[:rows] = own_ref[...]
    out_ref[rows:] = oth_ref[...]


def pair(own, oth, after):
    rows, width = own.shape
    return pl.pallas_call(
        pair_kernel,
        in_specs=[VMEM, VMEM, ANY],
        out_specs=VMEM,
        out_shape=jax.ShapeDtypeStruct((2 * rows, width), own.dtype),
        compiler_params=pltpu.CompilerParams(vmem_limit_bytes=4 * MIB),
    )(own, oth, after)


def gate_kernel(*refs):
    del refs


def gate(arrays, after, flops=0):
    count = len(arrays)
    return pl.pallas_call(
        gate_kernel,
        in_specs=[ANY] * (count + 1),
        out_specs=[ANY] * count,
        out_shape=[jax.ShapeDtypeStruct(array.shape, array.dtype) for array in arrays],
        input_output_aliases={at: at for at in range(count)},
        compiler_params=pltpu.CompilerParams(vmem_limit_bytes=MIB),
        cost_estimate=pl.CostEstimate(flops=flops, bytes_accessed=0, transcendentals=0),
    )(*arrays, after)


def arrange_kernel(y_ref, hi_ref, core_ref, own_ref, oth_ref, _, out_ref, sems):
    depth = own_ref.shape[0]
    block = own_ref.shape[1] // 16
    y, x_hi, core = y_ref[0], hi_ref[0], core_ref[0]

    def copy(at, side, ref):
        by, flip = at // 2, at % 2
        x_to = x_hi + flip - 2 * x_hi * flip
        first = (lax.rem(y + by, Y) * 4 + x_to * 2 + core) * block
        return pltpu.make_async_copy(
            ref.at[:, pl.ds(pl.multiple_of(first, HD), block)],
            out_ref.at[pl.ds(side * depth, depth), pl.ds(at * block, block)],
            sems.at[2 * at + side],
        )

    copies = [copy(at, side, ref) for at in range(8) for side, ref in enumerate((own_ref, oth_ref))]
    for one in copies:
        one.start()
    for one in copies:
        one.wait()


def arrange(own, oth, y, x_hi, core, after):
    depth, wide = own.shape
    smem = pl.BlockSpec(memory_space=pltpu.SMEM)
    return pl.pallas_call(
        arrange_kernel,
        in_specs=[smem, smem, smem, ANY, ANY, ANY],
        out_specs=VMEM,
        out_shape=jax.ShapeDtypeStruct((2 * depth, wide // 2), own.dtype),
        scratch_shapes=[pltpu.SemaphoreType.DMA((16,))],
        compiler_params=pltpu.CompilerParams(vmem_limit_bytes=8 * MIB),
        cost_estimate=pl.CostEstimate(flops=0, bytes_accessed=10**7, transcendentals=0),
    )(
        y.reshape(1),
        x_hi.reshape(1),
        core.reshape(1),
        pltpu.with_memory_space_constraint(own, pltpu.HBM),
        oth,
        after,
    )


def share_of(heads, weight_ref, by):
    return dot(heads, weight_ref[:, by * 6 * HD : (by + 1) * 6 * HD])


def both_of(own_ref, oth_ref):
    return jnp.concatenate([own_ref[...], oth_ref[...]], axis=1)


def far_kernel(own_ref, oth_ref, weight_ref, a_ref, b_ref):
    half = a_ref.shape[1]
    share = share_of(both_of(own_ref, oth_ref), weight_ref, 2)
    a_ref[...] = share[:, :half].astype(BF16)
    b_ref[...] = share[:, half:].astype(BF16)


def home_kernel(own_ref, oth_ref, weight_ref, out_ref):
    out_ref[...] = share_of(both_of(own_ref, oth_ref), weight_ref, 0)


def near_kernel(own_ref, oth_ref, weight_ref, a_ref, b_ref, up_ref, down_ref):
    half = a_ref.shape[1]
    heads = both_of(own_ref, oth_ref)
    share = share_of(heads, weight_ref, 1)
    up_ref[:, :half] = (share[:, :half] + a_ref[...].astype(F32)).astype(BF16)
    up_ref[:, half:] = share[:, half:].astype(BF16)
    share = share_of(heads, weight_ref, 3)
    down_ref[:, :half] = share[:, :half].astype(BF16)
    down_ref[:, half:] = (share[:, half:] + b_ref[...].astype(F32)).astype(BF16)


def sum_kernel(home_ref, up_ref, down_ref, own_ref, oth_ref):
    half = own_ref.shape[1]
    total = home_ref[...] + up_ref[...].astype(F32) + down_ref[...].astype(F32)
    own_ref[...] = total[:, :half]
    oth_ref[...] = total[:, half:].astype(BF16)


def projecting(kernel, out_shape, *operands):
    rows, depth = operands[0].shape
    return pl.pallas_call(
        kernel,
        out_shape=out_shape,
        compiler_params=pltpu.CompilerParams(vmem_limit_bytes=14 * MIB),
        cost_estimate=pl.CostEstimate(
            flops=16 * rows * depth * depth, bytes_accessed=2 * 10**6, transcendentals=0
        ),
    )(*operands)


def body(queries, new_keys, new_values, cache_keys, cache_values, out_weight):
    rows, width = queries.shape
    head_at = lax.axis_index("head").astype(jnp.int32)
    core, x_hi, y = head_at & 1, (head_at >> 1) & 1, head_at >> 2

    def along_z(array, by):
        return lax.ppermute(
            array, "ctx", [(x * Z + z, x * Z + (z + by) % Z) for x in range(2) for z in range(Z)]
        )

    def across_x(array):
        return lax.ppermute(array, "ctx", [(i, (i + Z) % (2 * Z)) for i in range(2 * Z)])

    def across_core(array):
        return lax.ppermute(array, "head", [(i, i ^ 1) for i in range(4 * Y)])

    def across_hi(array):
        return lax.ppermute(array, "head", [(i, i ^ 2) for i in range(4 * Y)])

    def along_y(array, by):
        return lax.ppermute(array, "head", [(i, (i + 4 * by) % (4 * Y)) for i in range(4 * Y)])

    def shape(*dims, dtype=BF16):
        return jax.ShapeDtypeStruct(dims, dtype)

    weight_oth = across_core(out_weight)
    q_here, *cached = ready(queries, cache_keys, new_keys, cache_values, new_values)
    q = {0: pair(q_here, across_x(queries), cached[0])}
    q[1], q[-1] = along_z(q[0], -1), along_z(q[0], 1)
    part = {}
    part[0], oth = attend([q[0]], *cached, after=q_here)
    ahead = [along_z(q[1], -1), along_z(q[-1], 1)]
    part[1], part[-1], oth = attend([q[1], q[-1]], *cached, more=oth)
    q[2], q[-2] = gate(ahead, part[1])
    ahead = [along_z(q[2], -1), along_z(q[-2], 1)]
    part[2], part[-2], near = attend([q[2], q[-2]], *cached, after=part[1])
    q[3], q[-3] = gate(ahead, part[2])
    ahead = along_z(q[3], -1)
    part[3], part[-3], far = attend([q[3], q[-3]], *cached, after=part[2])
    (q[4],) = gate([ahead], part[3])
    part[4], last = attend([q[4]], *cached, after=part[3])

    one = shape(rows + TAIL, width)

    def merged(theirs, *blocks):
        out = small(
            functools.partial(across_kernel, len(blocks)),
            [one] * len(blocks),
            *[part[d] for d in blocks],
            theirs,
        )
        part.update(zip(blocks, out))

    def met(there, here):
        return small(merge_kernel, one, there, here)

    oth = across_x(gate([oth], q[2])[0])
    near = across_x(gate([near], q[3])[0])
    far = across_x(gate([far], q[4])[0])
    weight = arrange(out_weight, weight_oth, y, x_hi, core, last)
    merged(gate([across_x(last)], weight)[0], 4)
    merged(gate([far], part[4])[0], 3, -3)
    merged(gate([near], part[3])[0], 2, -2)
    merged(gate([oth], part[2])[0], 1, -1, 0)
    up = met(along_z(part[4], 1), part[3])
    down = met(gate([along_z(part[-3], -1)], up)[0], part[-2])
    close = met(gate([along_z(part[2], 1)], down)[0], part[1])
    (up,) = gate([along_z(up, 3)], part[0], flops=10**10)
    back = [along_z(part[-1], -1), along_z(close, 1), along_z(down, -2), up]
    own = small(last_kernel, shape(rows, width), part[0], *back)

    oth = across_core(own)
    a, b = projecting(far_kernel, [shape(rows, width)] * 2, own, oth, weight)
    a, b = along_y(a, 1), along_y(b, -1)
    home = projecting(home_kernel, shape(rows, 2 * width, dtype=F32), own, oth, weight)
    up, down = projecting(near_kernel, [shape(rows, 2 * width)] * 2, own, oth, weight, a, b)
    ours, rest = small(
        sum_kernel,
        [shape(rows, width, dtype=F32), shape(rows, width)],
        home,
        along_y(up, 1),
        along_y(down, -1),
    )
    return ours + across_hi(rest).astype(F32)


def solution(mesh):
    placed = (
        P("ctx", "head"),
        P("ctx", "head"),
        P("ctx", "head"),
        P("ctx", "head"),
        P("ctx", "head"),
        P("head", None),
    )
    return jax.shard_map(
        body, mesh=mesh, in_specs=placed, out_specs=P("ctx", "head"), check_vma=False
    )
```

```python
import functools

import jax
import jax.numpy as jnp
from jax import lax
from jax.experimental import pallas as pl
from jax.experimental.pallas import tpu as pltpu
from jax.sharding import PartitionSpec as P

HD = 128
SCALE2 = HD ** (-0.5) * 1.4426950408889634
CHUNK = 512
TAIL = 16
LARGE = 2.0**100
MIB = 1024 * 1024
Z, Y = 8, 4
NT = (((1,), (1,)), ((), ()))
F32 = jnp.float32
BF16 = jnp.bfloat16
VMEM = pl.BlockSpec(memory_space=pltpu.VMEM)
ANY = pl.BlockSpec(memory_space=pl.ANY)
HBM = pl.BlockSpec(memory_space=pltpu.HBM)


def dot(a, b, dims=(((1,), (0,)), ((), ()))):
    return lax.dot_general(a, b, dims, preferred_element_type=F32)


def lse_rows(lse):
    at = lax.broadcasted_iota(jnp.int32, (8, HD), 0)
    row = jnp.broadcast_to(lse, (8, HD))
    hi = row.astype(BF16).astype(F32)
    mid = (row - hi).astype(BF16).astype(F32)
    out = jnp.where(at == 0, hi, jnp.where(at == 1, mid, jnp.where(at == 2, row - hi - mid, 0.0)))
    return jnp.concatenate([out, jnp.zeros((TAIL - 8, HD), F32)], axis=0).astype(BF16)


def lse_of(tail):
    parts = tail[0:3].astype(F32)
    return parts[0:1] + parts[1:2] + parts[2:3]


def attend_kernel(count, *refs):
    q_refs, refs = refs[:count], refs[count:]
    ck_ref, nk_ref, cvt_ref, nvt_ref, more_ref = refs[:5]
    own_refs, oth_ref = refs[5 : 5 + count], refs[5 + count]
    q_s, ot_s, lse_s, tot_s = refs[6 + count :]
    pair = q_refs[0].shape[0]
    rows = pair // 2
    wide = q_s.shape[0]
    groups = ck_ref.shape[1] // HD
    chunks = ck_ref.shape[0] // CHUNK
    for at, ref in enumerate(q_refs):
        q_s[at * pair : (at + 1) * pair] = ref[...]
    if wide > count * pair:
        q_s[count * pair :] = jnp.zeros((wide - count * pair, q_s.shape[1]), BF16)

    def cols_of(h):
        return pl.ds(pl.multiple_of(h * HD, HD), HD)

    steps = [(h, at) for h in range(groups) for at in range(-1, chunks)]

    def scores(h, at):
        cols = slice(h * HD, (h + 1) * HD)
        keys = nk_ref[:, cols] if at < 0 else ck_ref[at * CHUNK : (at + 1) * CHUNK, cols]
        return dot(keys, q_s[:, cols], NT)

    ahead = scores(*steps[0])
    for index, (h, at) in enumerate(steps):
        s = ahead
        if index + 1 < len(steps):
            ahead = scores(*steps[index + 1])
        cols = slice(h * HD, (h + 1) * HD)
        if at < 0:
            shift = jnp.max(s, axis=0, keepdims=True) * SCALE2
        p = jnp.exp2(s * SCALE2 - shift)
        values = nvt_ref[cols, :] if at < 0 else cvt_ref[cols, at * CHUNK : (at + 1) * CHUNK]
        more = dot(values, p.astype(BF16))
        total = jnp.sum(p, axis=0, keepdims=True) + (0.0 if at < 0 else total)
        o = more if at < 0 else o + more
        if at == chunks - 1:
            ot_s[h] = o * (1.0 / total)
            lse_s[h] = jnp.broadcast_to(shift + jnp.log2(total), (8, wide))
            tot_s[h] = jnp.broadcast_to(total, (8, wide))

    fits = jnp.min(jnp.where(tot_s[...] <= LARGE, 1.0, 0.0))

    @pl.when(fits < 0.5)
    def _():
        def careful(h, _):
            cols = cols_of(h)
            q = q_s[:, cols]
            s_new = dot(nk_ref[:, cols], q, NT)

            def chunk_at(j):
                return pl.ds(pl.multiple_of(j * HD, HD), HD)

            def peak_of(j, peak):
                s = dot(ck_ref[chunk_at(j), cols], q, NT)
                return jnp.maximum(peak, jnp.max(s, axis=0, keepdims=True))

            turns = ck_ref.shape[0] // HD
            peak = lax.fori_loop(0, turns, peak_of, jnp.max(s_new, axis=0, keepdims=True))
            p = jnp.exp2((s_new - peak) * SCALE2)
            ot_s[h] = dot(nvt_ref[cols, :], p.astype(BF16))

            def add(j, total):
                s = dot(ck_ref[chunk_at(j), cols], q, NT)
                p = jnp.exp2((s - peak) * SCALE2)
                ot_s[h] += dot(cvt_ref[cols, chunk_at(j)], p.astype(BF16))
                return total + jnp.sum(p, axis=0, keepdims=True)

            total = lax.fori_loop(0, turns, add, jnp.sum(p, axis=0, keepdims=True))
            ot_s[h] = ot_s[h] * (1.0 / total)
            lse_s[h] = jnp.broadcast_to(peak * SCALE2 + jnp.log2(total), (8, wide))
            return 0

        lax.fori_loop(0, groups, careful, 0)

    each = rows + TAIL
    if oth_ref.shape[0] > count * each:
        oth_ref[count * each :] = more_ref[...]
    for h in range(groups):
        cols = slice(h * HD, (h + 1) * HD)
        o = ot_s[h].T.astype(BF16)
        lse = lse_s[h]
        for at, ref in enumerate(own_refs):
            for side, (to, base) in enumerate(((ref, 0), (oth_ref, at * each))):
                begin = at * pair + side * rows
                to[base : base + rows, cols] = o[begin : begin + rows]
                turned = pltpu.roll(lse, wide - begin, axis=1) if begin else lse
                to[base + rows : base + each, cols] = lse_rows(turned[0:1, :HD])


def attend(blocks, ck, nk, cvt, nvt, more=None, after=None):
    count = len(blocks)
    pair, width = blocks[0].shape
    wide = -(-count * pair // HD) * HD
    groups = width // HD
    keys = ck.shape[0] + nk.shape[0]
    each = pair // 2 + TAIL
    extra = 0 if more is None else more.shape[0]
    last = (after if more is None else more, ANY if more is None else VMEM)
    return pl.pallas_call(
        functools.partial(attend_kernel, count),
        in_specs=[VMEM] * (count + 4) + [last[1]],
        out_specs=[VMEM] * (count + 1),
        out_shape=[jax.ShapeDtypeStruct((each, width), BF16)] * count
        + [jax.ShapeDtypeStruct((count * each + extra, width), BF16)],
        scratch_shapes=[
            pltpu.VMEM((wide, width), BF16),
            pltpu.VMEM((groups, HD, wide), F32),
            pltpu.VMEM((groups, 8, wide), F32),
            pltpu.VMEM((groups, 8, wide), F32),
        ],
        compiler_params=pltpu.CompilerParams(vmem_limit_bytes=24 * MIB),
        cost_estimate=pl.CostEstimate(
            flops=12 * wide * keys * width, bytes_accessed=10**6, transcendentals=0
        ),
    )(*blocks, ck, nk, cvt, nvt, last[0])


def merged_heads(blocks):
    rows = blocks[0].shape[0] - TAIL
    groups = blocks[0].shape[1] // HD
    lses = [lse_of(block[rows:]) for block in blocks]
    high = functools.reduce(jnp.maximum, lses)
    weights = [jnp.exp2(lse - high) for lse in lses]
    total = functools.reduce(jnp.add, weights)
    lse = high + jnp.log2(total)
    packed = [weight / total for weight in weights]
    packed = [share[:, h * HD : (h + 1) * HD] for share in packed for h in range(groups)]
    square = jnp.concatenate(packed + [jnp.zeros((HD - len(packed), HD), F32)], axis=0).T
    for h in range(groups):
        cols = slice(h * HD, (h + 1) * HD)
        merged = 0.0
        for at, block in enumerate(blocks):
            column = at * groups + h
            merged += square[:rows, column : column + 1] * block[:rows, cols].astype(F32)
        yield cols, merged, lse[:, cols]


def merge_kernel(*refs):
    out_ref = refs[-1]
    rows = out_ref.shape[0] - TAIL
    for cols, merged, lse in merged_heads([ref[...] for ref in refs[:-1]]):
        out_ref[:rows, cols] = merged.astype(BF16)
        out_ref[rows:, cols] = lse_rows(lse)


def across_kernel(count, *refs):
    mine, theirs_ref, outs = refs[:count], refs[count], refs[count + 1 :]
    each = outs[0].shape[0]
    for at, (mine_ref, out_ref) in enumerate(zip(mine, outs)):
        for cols, merged, lse in merged_heads(
            [mine_ref[...], theirs_ref[at * each : (at + 1) * each]]
        ):
            out_ref[: each - TAIL, cols] = merged.astype(BF16)
            out_ref[each - TAIL :, cols] = lse_rows(lse)


def last_kernel(*refs):
    for cols, merged, _ in merged_heads([ref[...] for ref in refs[:-1]]):
        refs[-1][:, cols] = merged.astype(BF16)


def small(kernel, out_shape, *operands):
    return pl.pallas_call(
        kernel,
        out_shape=out_shape,
        compiler_params=pltpu.CompilerParams(vmem_limit_bytes=6 * MIB),
        cost_estimate=pl.CostEstimate(flops=1, bytes_accessed=1, transcendentals=0),
    )(*operands)


def ready_kernel(q_in, ck_in, nk_in, cv_in, nv_in, q_ref, ck_ref, nk_ref, cvt_ref, nvt_ref, cv_s, nv_s, sems):
    chunks = cv_in.shape[0] // CHUNK
    parts = [pl.ds(at * CHUNK, CHUNK) for at in range(chunks)]
    moves = [(cv_in.at[part], cv_s.at[part]) for part in parts]
    moves += [(nv_in, nv_s), (ck_in, ck_ref), (nk_in, nk_ref), (q_in, q_ref)]
    copies = [pltpu.make_async_copy(a, b, sems.at[at]) for at, (a, b) in enumerate(moves)]
    for copy in copies:
        copy.start()
    for at in range(chunks):
        copies[at].wait()
        for h in range(cv_in.shape[1] // HD):
            cols = slice(h * HD, (h + 1) * HD)
            cvt_ref[cols, at * CHUNK : (at + 1) * CHUNK] = cv_s[at * CHUNK : (at + 1) * CHUNK, cols].T
    copies[chunks].wait()
    for h in range(cv_in.shape[1] // HD):
        cols = slice(h * HD, (h + 1) * HD)
        nvt_ref[cols, :] = nv_s[:, cols].T
    for copy in copies[chunks + 1 :]:
        copy.wait()


def ready(q, ck, nk, cv, nv):
    shapes = [q.shape, ck.shape, nk.shape, cv.shape[::-1], nv.shape[::-1]]
    return pl.pallas_call(
        ready_kernel,
        in_specs=[HBM] * 5,
        out_specs=[VMEM] * 5,
        out_shape=[jax.ShapeDtypeStruct(shape, BF16) for shape in shapes],
        scratch_shapes=[
            pltpu.VMEM(cv.shape, BF16),
            pltpu.VMEM(nv.shape, BF16),
            pltpu.SemaphoreType.DMA((cv.shape[0] // CHUNK + 4,)),
        ],
        compiler_params=pltpu.CompilerParams(vmem_limit_bytes=12 * MIB),
        cost_estimate=pl.CostEstimate(flops=0, bytes_accessed=7 * 10**6, transcendentals=0),
    )(*[pltpu.with_memory_space_constraint(array, pltpu.HBM) for array in (q, ck, nk, cv, nv)])


def pair_kernel(own_ref, oth_ref, _, out_ref):
    rows = own_ref.shape[0]
    out_ref[:rows] = own_ref[...]
    out_ref[rows:] = oth_ref[...]


def pair(own, oth, after):
    rows, width = own.shape
    return pl.pallas_call(
        pair_kernel,
        in_specs=[VMEM, VMEM, ANY],
        out_specs=VMEM,
        out_shape=jax.ShapeDtypeStruct((2 * rows, width), own.dtype),
        compiler_params=pltpu.CompilerParams(vmem_limit_bytes=4 * MIB),
    )(own, oth, after)


def gate_kernel(*refs):
    del refs


def gate(arrays, after, flops=0):
    count = len(arrays)
    return pl.pallas_call(
        gate_kernel,
        in_specs=[ANY] * (count + 1),
        out_specs=[ANY] * count,
        out_shape=[jax.ShapeDtypeStruct(array.shape, array.dtype) for array in arrays],
        input_output_aliases={at: at for at in range(count)},
        compiler_params=pltpu.CompilerParams(vmem_limit_bytes=MIB),
        cost_estimate=pl.CostEstimate(flops=flops, bytes_accessed=0, transcendentals=0),
    )(*arrays, after)


def arrange_kernel(core_ref, own_ref, oth_ref, _, out_ref, sems):
    depth = own_ref.shape[0]
    block = own_ref.shape[1] // 16
    core = core_ref[0]

    def copy(at, side, ref):
        first = (2 * at + core) * block
        return pltpu.make_async_copy(
            ref.at[:, pl.ds(pl.multiple_of(first, HD), block)],
            out_ref.at[pl.ds(side * depth, depth), pl.ds(at * block, block)],
            sems.at[2 * at + side],
        )

    copies = [copy(at, side, ref) for at in range(8) for side, ref in enumerate((own_ref, oth_ref))]
    for one in copies:
        one.start()
    for one in copies:
        one.wait()


def arrange(own, oth, core, after):
    depth, wide = own.shape
    smem = pl.BlockSpec(memory_space=pltpu.SMEM)
    return pl.pallas_call(
        arrange_kernel,
        in_specs=[smem, ANY, ANY, ANY],
        out_specs=VMEM,
        out_shape=jax.ShapeDtypeStruct((2 * depth, wide // 2), own.dtype),
        scratch_shapes=[pltpu.SemaphoreType.DMA((16,))],
        compiler_params=pltpu.CompilerParams(vmem_limit_bytes=8 * MIB),
        cost_estimate=pl.CostEstimate(flops=0, bytes_accessed=10**7, transcendentals=0),
    )(
        core.reshape(1),
        pltpu.with_memory_space_constraint(own, pltpu.HBM),
        oth,
        after,
    )


def project_kernel(own_ref, oth_ref, weight_ref, out_ref):
    heads = jnp.concatenate([own_ref[...], oth_ref[...]], axis=1)
    width = own_ref.shape[1]
    for at in range(0, out_ref.shape[0], 2):
        share = dot(heads, weight_ref[:, at * width : (at + 2) * width]).astype(BF16)
        out_ref[at] = share[:, :width]
        out_ref[at + 1] = share[:, width:]


def projecting(kernel, out_shape, *operands):
    rows, depth = operands[0].shape
    return pl.pallas_call(
        kernel,
        out_shape=out_shape,
        compiler_params=pltpu.CompilerParams(vmem_limit_bytes=14 * MIB),
        cost_estimate=pl.CostEstimate(
            flops=16 * rows * depth * depth, bytes_accessed=2 * 10**6, transcendentals=0
        ),
    )(*operands)


def body(queries, new_keys, new_values, cache_keys, cache_values, out_weight):
    rows, width = queries.shape
    head_at = lax.axis_index("head").astype(jnp.int32)
    core = head_at & 1

    def along_z(array, by):
        return lax.ppermute(
            array, "ctx", [(x * Z + z, x * Z + (z + by) % Z) for x in range(2) for z in range(Z)]
        )

    def across_x(array):
        return lax.ppermute(array, "ctx", [(i, (i + Z) % (2 * Z)) for i in range(2 * Z)])

    def across_core(array):
        return lax.ppermute(array, "head", [(i, i ^ 1) for i in range(4 * Y)])

    def shape(*dims, dtype=BF16):
        return jax.ShapeDtypeStruct(dims, dtype)

    weight_oth = across_core(out_weight)
    q_here, *cached = ready(queries, cache_keys, new_keys, cache_values, new_values)
    q = {0: pair(q_here, across_x(queries), cached[0])}
    q[1], q[-1] = along_z(q[0], -1), along_z(q[0], 1)
    part = {}
    part[0], oth = attend([q[0]], *cached, after=q_here)
    ahead = [along_z(q[1], -1), along_z(q[-1], 1)]
    part[1], part[-1], oth = attend([q[1], q[-1]], *cached, more=oth)
    q[2], q[-2] = gate(ahead, part[1])
    ahead = [along_z(q[2], -1), along_z(q[-2], 1)]
    part[2], part[-2], near = attend([q[2], q[-2]], *cached, after=part[1])
    q[3], q[-3] = gate(ahead, part[2])
    ahead = along_z(q[3], -1)
    part[3], part[-3], far = attend([q[3], q[-3]], *cached, after=part[2])
    (q[4],) = gate([ahead], part[3])
    part[4], last = attend([q[4]], *cached, after=part[3])

    one = shape(rows + TAIL, width)

    def merged(theirs, *blocks):
        out = small(
            functools.partial(across_kernel, len(blocks)),
            [one] * len(blocks),
            *[part[d] for d in blocks],
            theirs,
        )
        part.update(zip(blocks, out))

    def met(there, here):
        return small(merge_kernel, one, there, here)

    oth = across_x(gate([oth], q[2])[0])
    near = across_x(gate([near], q[3])[0])
    far = across_x(gate([far], q[4])[0])
    weight = arrange(out_weight, weight_oth, core, last)
    merged(gate([across_x(last)], weight)[0], 4)
    merged(gate([far], part[4])[0], 3, -3)
    merged(gate([near], part[3])[0], 2, -2)
    merged(gate([oth], part[2])[0], 1, -1, 0)
    up = met(along_z(part[4], 1), part[3])
    down = met(gate([along_z(part[-3], -1)], up)[0], part[-2])
    close = met(gate([along_z(part[2], 1)], down)[0], part[1])
    (up,) = gate([along_z(up, 3)], part[0], flops=10**10)
    back = [along_z(part[-1], -1), along_z(close, 1), along_z(down, -2), up]
    own = small(last_kernel, shape(rows, width), part[0], *back)

    oth = across_core(own)
    shares = projecting(project_kernel, shape(2 * Y, rows, width), own, oth, weight)
    groups = [[2 * at + side for at in range(2 * Y)] for side in range(2)]
    shares = lax.all_to_all(shares, "head", 0, 0, axis_index_groups=groups, tiled=True)
    return jnp.sum(shares.astype(F32), axis=0)


def solution(mesh):
    placed = (
        P("ctx", "head"),
        P("ctx", "head"),
        P("ctx", "head"),
        P("ctx", "head"),
        P("ctx", "head"),
        P("head", None),
    )
    return jax.shard_map(
        body, mesh=mesh, in_specs=placed, out_specs=P("ctx", "head"), check_vma=False
    )
```

```python
import functools

import jax
import jax.numpy as jnp
from jax import lax
from jax.experimental import pallas as pl
from jax.experimental.pallas import tpu as pltpu
from jax.sharding import PartitionSpec as P

HD = 128
SCALE2 = HD ** (-0.5) * 1.4426950408889634
CHUNK = 512
TAIL = 16
LARGE = 2.0**100
MIB = 1024 * 1024
Z, Y = 8, 4
NT = (((1,), (1,)), ((), ()))
F32 = jnp.float32
BF16 = jnp.bfloat16
VMEM = pl.BlockSpec(memory_space=pltpu.VMEM)
ANY = pl.BlockSpec(memory_space=pl.ANY)
HBM = pl.BlockSpec(memory_space=pltpu.HBM)


def dot(a, b, dims=(((1,), (0,)), ((), ()))):
    return lax.dot_general(a, b, dims, preferred_element_type=F32)


def lse_rows(lse):
    at = lax.broadcasted_iota(jnp.int32, (8, HD), 0)
    row = jnp.broadcast_to(lse, (8, HD))
    hi = row.astype(BF16).astype(F32)
    mid = (row - hi).astype(BF16).astype(F32)
    out = jnp.where(at == 0, hi, jnp.where(at == 1, mid, jnp.where(at == 2, row - hi - mid, 0.0)))
    return jnp.concatenate([out, jnp.zeros((TAIL - 8, HD), F32)], axis=0).astype(BF16)


def lse_of(tail):
    parts = tail[0:3].astype(F32)
    return parts[0:1] + parts[1:2] + parts[2:3]


def attend_kernel(count, looped, *refs):
    q_refs, refs = refs[:count], refs[count:]
    ck_ref, nk_ref, cvt_ref, nvt_ref, more_ref = refs[:5]
    own_refs, oth_ref = refs[5 : 5 + count], refs[5 + count]
    q_s, ot_s, lse_s, tot_s = refs[6 + count :]
    pair = q_refs[0].shape[0]
    rows = pair // 2
    wide = q_s.shape[0]
    groups = ck_ref.shape[1] // HD
    chunks = ck_ref.shape[0] // CHUNK
    for at, ref in enumerate(q_refs):
        q_s[at * pair : (at + 1) * pair] = ref[...]
    if wide > count * pair:
        q_s[count * pair :] = jnp.zeros((wide - count * pair, q_s.shape[1]), BF16)

    def cols_of(h):
        if isinstance(h, int):
            return slice(h * HD, (h + 1) * HD)
        return pl.ds(pl.multiple_of(h * HD, HD), HD)

    def sequence(heads):
        steps = [(h, at) for h in heads for at in range(-1, chunks)]

        def scores(h, at):
            keys = nk_ref[:, cols_of(h)] if at < 0 else ck_ref[at * CHUNK : (at + 1) * CHUNK, cols_of(h)]
            return dot(keys, q_s[:, cols_of(h)], NT)

        ahead = scores(*steps[0])
        for index, (h, at) in enumerate(steps):
            s = ahead
            if index + 1 < len(steps):
                ahead = scores(*steps[index + 1])
            if at < 0:
                shift = jnp.max(s, axis=0, keepdims=True) * SCALE2
            p = jnp.exp2(s * SCALE2 - shift)
            values = (
                nvt_ref[cols_of(h), :]
                if at < 0
                else cvt_ref[cols_of(h), at * CHUNK : (at + 1) * CHUNK]
            )
            more = dot(values, p.astype(BF16))
            total = jnp.sum(p, axis=0, keepdims=True) + (0.0 if at < 0 else total)
            o = more if at < 0 else o + more
            if at == chunks - 1:
                ot_s[h] = o * (1.0 / total)
                lse_s[h] = jnp.broadcast_to(shift + jnp.log2(total), (8, wide))
                tot_s[h] = jnp.broadcast_to(total, (8, wide))

    if looped:
        pl.loop(0, groups)(lambda h: sequence([h]))
    else:
        sequence(range(groups))

    fits = jnp.min(jnp.where(tot_s[...] <= LARGE, 1.0, 0.0))

    @pl.when(fits < 0.5)
    def _():
        def careful(h, _):
            cols = cols_of(h)
            q = q_s[:, cols]
            s_new = dot(nk_ref[:, cols], q, NT)

            def chunk_at(j):
                return pl.ds(pl.multiple_of(j * HD, HD), HD)

            def peak_of(j, peak):
                s = dot(ck_ref[chunk_at(j), cols], q, NT)
                return jnp.maximum(peak, jnp.max(s, axis=0, keepdims=True))

            turns = ck_ref.shape[0] // HD
            peak = lax.fori_loop(0, turns, peak_of, jnp.max(s_new, axis=0, keepdims=True))
            p = jnp.exp2((s_new - peak) * SCALE2)
            ot_s[h] = dot(nvt_ref[cols, :], p.astype(BF16))

            def add(j, total):
                s = dot(ck_ref[chunk_at(j), cols], q, NT)
                p = jnp.exp2((s - peak) * SCALE2)
                ot_s[h] += dot(cvt_ref[cols, chunk_at(j)], p.astype(BF16))
                return total + jnp.sum(p, axis=0, keepdims=True)

            total = lax.fori_loop(0, turns, add, jnp.sum(p, axis=0, keepdims=True))
            ot_s[h] = ot_s[h] * (1.0 / total)
            lse_s[h] = jnp.broadcast_to(peak * SCALE2 + jnp.log2(total), (8, wide))
            return 0

        lax.fori_loop(0, groups, careful, 0)

    each = rows + TAIL
    if oth_ref.shape[0] > count * each:
        oth_ref[count * each :] = more_ref[...]

    @pl.loop(0, groups)
    def _(h):
        cols = cols_of(h)
        o = ot_s[h].T.astype(BF16)
        lse = lse_s[h]
        for at, ref in enumerate(own_refs):
            for side, (to, base) in enumerate(((ref, 0), (oth_ref, at * each))):
                begin = at * pair + side * rows
                to[base : base + rows, cols] = o[begin : begin + rows]
                turned = pltpu.roll(lse, wide - begin, axis=1) if begin else lse
                to[base + rows : base + each, cols] = lse_rows(turned[0:1, :HD])


def attend(blocks, ck, nk, cvt, nvt, more=None, after=None, looped=False):
    count = len(blocks)
    pair, width = blocks[0].shape
    wide = -(-count * pair // HD) * HD
    groups = width // HD
    keys = ck.shape[0] + nk.shape[0]
    each = pair // 2 + TAIL
    extra = 0 if more is None else more.shape[0]
    last = (after if more is None else more, ANY if more is None else VMEM)
    return pl.pallas_call(
        functools.partial(attend_kernel, count, looped),
        in_specs=[VMEM] * (count + 4) + [last[1]],
        out_specs=[VMEM] * (count + 1),
        out_shape=[jax.ShapeDtypeStruct((each, width), BF16)] * count
        + [jax.ShapeDtypeStruct((count * each + extra, width), BF16)],
        scratch_shapes=[
            pltpu.VMEM((wide, width), BF16),
            pltpu.VMEM((groups, HD, wide), F32),
            pltpu.VMEM((groups, 8, wide), F32),
            pltpu.VMEM((groups, 8, wide), F32),
        ],
        compiler_params=pltpu.CompilerParams(vmem_limit_bytes=24 * MIB),
        cost_estimate=pl.CostEstimate(
            flops=12 * wide * keys * width, bytes_accessed=10**6, transcendentals=0
        ),
    )(*blocks, ck, nk, cvt, nvt, last[0])


def merged_heads(blocks):
    rows = blocks[0].shape[0] - TAIL
    groups = blocks[0].shape[1] // HD
    lses = [lse_of(block[rows:]) for block in blocks]
    high = functools.reduce(jnp.maximum, lses)
    weights = [jnp.exp2(lse - high) for lse in lses]
    total = functools.reduce(jnp.add, weights)
    lse = high + jnp.log2(total)
    packed = [weight / total for weight in weights]
    packed = [share[:, h * HD : (h + 1) * HD] for share in packed for h in range(groups)]
    square = jnp.concatenate(packed + [jnp.zeros((HD - len(packed), HD), F32)], axis=0).T
    for h in range(groups):
        cols = slice(h * HD, (h + 1) * HD)
        merged = 0.0
        for at, block in enumerate(blocks):
            column = at * groups + h
            merged += square[:rows, column : column + 1] * block[:rows, cols].astype(F32)
        yield cols, merged, lse[:, cols]


def merge_kernel(*refs):
    out_ref = refs[-1]
    rows = out_ref.shape[0] - TAIL
    for cols, merged, lse in merged_heads([ref[...] for ref in refs[:-1]]):
        out_ref[:rows, cols] = merged.astype(BF16)
        out_ref[rows:, cols] = lse_rows(lse)


def across_kernel(count, *refs):
    mine, theirs_ref, outs = refs[:count], refs[count], refs[count + 1 :]
    each = outs[0].shape[0]
    for at, (mine_ref, out_ref) in enumerate(zip(mine, outs)):
        for cols, merged, lse in merged_heads(
            [mine_ref[...], theirs_ref[at * each : (at + 1) * each]]
        ):
            out_ref[: each - TAIL, cols] = merged.astype(BF16)
            out_ref[each - TAIL :, cols] = lse_rows(lse)


def last_kernel(*refs):
    for cols, merged, _ in merged_heads([ref[...] for ref in refs[:-1]]):
        refs[-1][:, cols] = merged.astype(BF16)


def small(kernel, out_shape, *operands):
    return pl.pallas_call(
        kernel,
        out_shape=out_shape,
        compiler_params=pltpu.CompilerParams(vmem_limit_bytes=6 * MIB),
        cost_estimate=pl.CostEstimate(flops=1, bytes_accessed=1, transcendentals=0),
    )(*operands)


def ready_kernel(q_in, ck_in, nk_in, cv_in, nv_in, q_ref, ck_ref, nk_ref, cvt_ref, nvt_ref, cv_s, nv_s, sems):
    chunks = cv_in.shape[0] // CHUNK
    parts = [pl.ds(at * CHUNK, CHUNK) for at in range(chunks)]
    moves = [(cv_in.at[part], cv_s.at[part]) for part in parts]
    moves += [(nv_in, nv_s), (ck_in, ck_ref), (nk_in, nk_ref), (q_in, q_ref)]
    copies = [pltpu.make_async_copy(a, b, sems.at[at]) for at, (a, b) in enumerate(moves)]
    for copy in copies:
        copy.start()
    for at in range(chunks):
        copies[at].wait()
        @pl.loop(0, cv_in.shape[1] // HD)
        def _(h):
            cols = pl.ds(pl.multiple_of(h * HD, HD), HD)
            cvt_ref[cols, at * CHUNK : (at + 1) * CHUNK] = cv_s[at * CHUNK : (at + 1) * CHUNK, cols].T

    copies[chunks].wait()
    for h in range(cv_in.shape[1] // HD):
        cols = slice(h * HD, (h + 1) * HD)
        nvt_ref[cols, :] = nv_s[:, cols].T
    for copy in copies[chunks + 1 :]:
        copy.wait()


def ready(q, ck, nk, cv, nv):
    shapes = [q.shape, ck.shape, nk.shape, cv.shape[::-1], nv.shape[::-1]]
    return pl.pallas_call(
        ready_kernel,
        in_specs=[HBM] * 5,
        out_specs=[VMEM] * 5,
        out_shape=[jax.ShapeDtypeStruct(shape, BF16) for shape in shapes],
        scratch_shapes=[
            pltpu.VMEM(cv.shape, BF16),
            pltpu.VMEM(nv.shape, BF16),
            pltpu.SemaphoreType.DMA((cv.shape[0] // CHUNK + 4,)),
        ],
        compiler_params=pltpu.CompilerParams(vmem_limit_bytes=12 * MIB),
        cost_estimate=pl.CostEstimate(flops=0, bytes_accessed=7 * 10**6, transcendentals=0),
    )(*[pltpu.with_memory_space_constraint(array, pltpu.HBM) for array in (q, ck, nk, cv, nv)])


def pair_kernel(own_ref, oth_ref, _, out_ref):
    rows = own_ref.shape[0]
    out_ref[:rows] = own_ref[...]
    out_ref[rows:] = oth_ref[...]


def pair(own, oth, after):
    rows, width = own.shape
    return pl.pallas_call(
        pair_kernel,
        in_specs=[VMEM, VMEM, ANY],
        out_specs=VMEM,
        out_shape=jax.ShapeDtypeStruct((2 * rows, width), own.dtype),
        compiler_params=pltpu.CompilerParams(vmem_limit_bytes=4 * MIB),
    )(own, oth, after)


def gate_kernel(*refs):
    del refs


def gate(arrays, after, flops=0):
    count = len(arrays)
    return pl.pallas_call(
        gate_kernel,
        in_specs=[ANY] * (count + 1),
        out_specs=[ANY] * count,
        out_shape=[jax.ShapeDtypeStruct(array.shape, array.dtype) for array in arrays],
        input_output_aliases={at: at for at in range(count)},
        compiler_params=pltpu.CompilerParams(vmem_limit_bytes=MIB),
        cost_estimate=pl.CostEstimate(flops=flops, bytes_accessed=0, transcendentals=0),
    )(*arrays, after)


def arrange_kernel(y_ref, hi_ref, core_ref, own_ref, oth_ref, _, out_ref, sems):
    depth = own_ref.shape[0]
    block = own_ref.shape[1] // 16
    y, x_hi, core = y_ref[0], hi_ref[0], core_ref[0]

    def copy(at, side, ref):
        by, flip = at // 2, at % 2
        x_to = x_hi + flip - 2 * x_hi * flip
        first = (lax.rem(y + by, Y) * 4 + x_to * 2 + core) * block
        return pltpu.make_async_copy(
            ref.at[:, pl.ds(pl.multiple_of(first, HD), block)],
            out_ref.at[pl.ds(side * depth, depth), pl.ds(at * block, block)],
            sems.at[2 * at + side],
        )

    copies = [copy(at, side, ref) for at in range(8) for side, ref in enumerate((own_ref, oth_ref))]
    for one in copies:
        one.start()
    for one in copies:
        one.wait()


def arrange(own, oth, y, x_hi, core, after):
    depth, wide = own.shape
    smem = pl.BlockSpec(memory_space=pltpu.SMEM)
    return pl.pallas_call(
        arrange_kernel,
        in_specs=[smem, smem, smem, ANY, ANY, ANY],
        out_specs=VMEM,
        out_shape=jax.ShapeDtypeStruct((2 * depth, wide // 2), own.dtype),
        scratch_shapes=[pltpu.SemaphoreType.DMA((16,))],
        compiler_params=pltpu.CompilerParams(vmem_limit_bytes=8 * MIB),
        cost_estimate=pl.CostEstimate(flops=0, bytes_accessed=10**7, transcendentals=0),
    )(
        y.reshape(1),
        x_hi.reshape(1),
        core.reshape(1),
        pltpu.with_memory_space_constraint(own, pltpu.HBM),
        oth,
        after,
    )


def share_of(heads, weight_ref, by):
    return dot(heads, weight_ref[:, by * 6 * HD : (by + 1) * 6 * HD])


def both_of(own_ref, oth_ref):
    return jnp.concatenate([own_ref[...], oth_ref[...]], axis=1)


def far_kernel(own_ref, oth_ref, weight_ref, a_ref, b_ref):
    half = a_ref.shape[1]
    share = share_of(both_of(own_ref, oth_ref), weight_ref, 2)
    a_ref[...] = share[:, :half].astype(BF16)
    b_ref[...] = share[:, half:].astype(BF16)


def near_kernel(own_ref, oth_ref, weight_ref, up_ref, up_rest_ref, down_ref, down_rest_ref):
    half = up_ref.shape[1]
    heads = both_of(own_ref, oth_ref)
    share = share_of(heads, weight_ref, 1)
    up_ref[...] = share[:, :half]
    up_rest_ref[...] = share[:, half:].astype(BF16)
    share = share_of(heads, weight_ref, 3)
    down_ref[...] = share[:, :half].astype(BF16)
    down_rest_ref[...] = share[:, half:]


def here_kernel(own_ref, oth_ref, weight_ref, out_ref, rest_ref):
    half = out_ref.shape[1]
    share = share_of(both_of(own_ref, oth_ref), weight_ref, 0)
    out_ref[...] = share[:, :half]
    rest_ref[...] = share[:, half:]


def sum_kernel(*refs):
    total = refs[0][...].astype(F32)
    for ref in refs[1:-1]:
        total += ref[...].astype(F32)
    refs[-1][...] = total.astype(refs[-1].dtype)


def projecting(kernel, out_shape, *operands):
    rows, depth = operands[0].shape
    return pl.pallas_call(
        kernel,
        out_shape=out_shape,
        compiler_params=pltpu.CompilerParams(vmem_limit_bytes=14 * MIB),
        cost_estimate=pl.CostEstimate(
            flops=16 * rows * depth * depth, bytes_accessed=2 * 10**6, transcendentals=0
        ),
    )(*operands)


def body(queries, new_keys, new_values, cache_keys, cache_values, out_weight):
    rows, width = queries.shape
    head_at = lax.axis_index("head").astype(jnp.int32)
    core, x_hi, y = head_at & 1, (head_at >> 1) & 1, head_at >> 2

    def along_z(array, by):
        return lax.ppermute(
            array, "ctx", [(x * Z + z, x * Z + (z + by) % Z) for x in range(2) for z in range(Z)]
        )

    def across_x(array):
        return lax.ppermute(array, "ctx", [(i, (i + Z) % (2 * Z)) for i in range(2 * Z)])

    def across_core(array):
        return lax.ppermute(array, "head", [(i, i ^ 1) for i in range(4 * Y)])

    def across_hi(array):
        return lax.ppermute(array, "head", [(i, i ^ 2) for i in range(4 * Y)])

    def along_y(array, by):
        return lax.ppermute(array, "head", [(i, (i + 4 * by) % (4 * Y)) for i in range(4 * Y)])

    def shape(*dims, dtype=BF16):
        return jax.ShapeDtypeStruct(dims, dtype)

    weight_oth = across_core(out_weight)
    q_here, *cached = ready(queries, cache_keys, new_keys, cache_values, new_values)
    q = {0: pair(q_here, across_x(queries), cached[0])}
    q[1], q[-1] = along_z(q[0], -1), along_z(q[0], 1)
    part = {}
    part[0], oth = attend([q[0]], *cached, after=q_here, looped=True)
    ahead = [along_z(q[1], -1), along_z(q[-1], 1)]
    part[1], part[-1], oth = attend([q[1], q[-1]], *cached, more=oth)
    q[2], q[-2] = gate(ahead, part[1])
    ahead = [along_z(q[2], -1), along_z(q[-2], 1)]
    part[2], part[-2], near = attend([q[2], q[-2]], *cached, after=part[1])
    q[3], q[-3] = gate(ahead, part[2])
    ahead = along_z(q[3], -1)
    oth = across_x(gate([oth], q[2])[0])
    part[3], part[-3], far = attend([q[3], q[-3]], *cached, after=oth)
    (q[4],) = gate([ahead], part[3])
    near = across_x(gate([near], q[3])[0])
    part[4], last = attend([q[4]], *cached, after=near)

    one = shape(rows + TAIL, width)

    def merged(theirs, *blocks):
        out = small(
            functools.partial(across_kernel, len(blocks)),
            [one] * len(blocks),
            *[part[d] for d in blocks],
            theirs,
        )
        part.update(zip(blocks, out))

    def met(there, here):
        return small(merge_kernel, one, there, here)

    far = across_x(gate([far], last)[0])
    merged(gate([across_x(last)], part[0], flops=2 * 10**9)[0], 4)
    merged(gate([far], part[4])[0], 3, -3)
    merged(gate([near], part[3])[0], 2, -2)
    merged(gate([oth], part[2])[0], 1, -1, 0)
    up = met(along_z(part[4], 1), part[3])
    down = met(gate([along_z(part[-3], -1)], up)[0], part[-2])
    close = met(gate([along_z(part[2], 1)], down)[0], part[1])
    weight = arrange(out_weight, weight_oth, y, x_hi, core, close)
    (up,) = gate([along_z(up, 3)], weight, flops=10**10)
    back = [along_z(part[-1], -1), along_z(close, 1), along_z(down, -2), up]
    own = small(last_kernel, shape(rows, width), part[0], *back)

    oth = across_core(own)
    tile, wide = shape(rows, width), shape(rows, width, dtype=F32)
    a, b = projecting(far_kernel, [tile, tile], own, oth, weight)
    b, a = along_y(b, -1), along_y(a, 1)
    up, up_rest, down, down_rest = projecting(near_kernel, [wide, tile, tile, wide], own, oth, weight)
    (b,) = gate([b], up, flops=10**10)
    up_rest, down = along_y(up_rest, 1), along_y(down, -1)
    (up_rest,) = gate([up_rest], b, flops=2 * 10**10)
    (down,) = gate([down], b, flops=10**9)
    down_rest = small(sum_kernel, tile, down_rest, b)
    (a,) = gate([a], up_rest, flops=10**10)
    down_rest = along_y(down_rest, -1)
    up = along_y(small(sum_kernel, tile, up, a), 1)
    here, rest = projecting(here_kernel, [wide, wide], own, oth, weight)
    (down_rest,) = gate([down_rest], here, flops=4 * 10**10)
    rest = across_hi(small(sum_kernel, tile, rest, up_rest, down_rest))
    ours = small(sum_kernel, wide, here, up, down)
    return ours + rest.astype(F32)


def solution(mesh):
    placed = (
        P("ctx", "head"),
        P("ctx", "head"),
        P("ctx", "head"),
        P("ctx", "head"),
        P("ctx", "head"),
        P("head", None),
    )
    return jax.shard_map(
        body, mesh=mesh, in_specs=placed, out_specs=P("ctx", "head"), check_vma=False
    )
```

```python
import functools

import jax
import jax.numpy as jnp
from jax import lax
from jax.experimental import pallas as pl
from jax.experimental.pallas import tpu as pltpu
from jax.sharding import PartitionSpec as P

HD = 128
SCALE2 = HD ** (-0.5) * 1.4426950408889634
CHUNK = 512
TAIL = 16
LARGE = 2.0**100
MIB = 1024 * 1024
Z, Y = 8, 4
NT = (((1,), (1,)), ((), ()))
F32 = jnp.float32
BF16 = jnp.bfloat16
VMEM = pl.BlockSpec(memory_space=pltpu.VMEM)
ANY = pl.BlockSpec(memory_space=pl.ANY)
HBM = pl.BlockSpec(memory_space=pltpu.HBM)


def dot(a, b, dims=(((1,), (0,)), ((), ()))):
    return lax.dot_general(a, b, dims, preferred_element_type=F32)


def lse_rows(lse):
    at = lax.broadcasted_iota(jnp.int32, (8, HD), 0)
    row = jnp.broadcast_to(lse, (8, HD))
    hi = row.astype(BF16).astype(F32)
    mid = (row - hi).astype(BF16).astype(F32)
    out = jnp.where(at == 0, hi, jnp.where(at == 1, mid, jnp.where(at == 2, row - hi - mid, 0.0)))
    return jnp.concatenate([out, jnp.zeros((TAIL - 8, HD), F32)], axis=0).astype(BF16)


def lse_of(tail):
    parts = tail[0:3].astype(F32)
    return parts[0:1] + parts[1:2] + parts[2:3]


def attend_kernel(count, looped, *refs):
    q_refs, refs = refs[:count], refs[count:]
    ck_ref, nk_ref, cvt_ref, nvt_ref, more_ref = refs[:5]
    own_refs, oth_ref = refs[5 : 5 + count], refs[5 + count]
    q_s, ot_s, lse_s, tot_s = refs[6 + count :]
    pair = q_refs[0].shape[0]
    rows = pair // 2
    wide = q_s.shape[0]
    groups = ck_ref.shape[1] // HD
    chunks = ck_ref.shape[0] // CHUNK
    for at, ref in enumerate(q_refs):
        q_s[at * pair : (at + 1) * pair] = ref[...]
    if wide > count * pair:
        q_s[count * pair :] = jnp.zeros((wide - count * pair, q_s.shape[1]), BF16)

    def cols_of(h):
        if isinstance(h, int):
            return slice(h * HD, (h + 1) * HD)
        return pl.ds(pl.multiple_of(h * HD, HD), HD)

    def sequence(heads):
        steps = [(h, at) for h in heads for at in range(-1, chunks)]

        def scores(h, at):
            keys = nk_ref[:, cols_of(h)] if at < 0 else ck_ref[at * CHUNK : (at + 1) * CHUNK, cols_of(h)]
            return dot(keys, q_s[:, cols_of(h)], NT)

        ahead = scores(*steps[0])
        for index, (h, at) in enumerate(steps):
            s = ahead
            if index + 1 < len(steps):
                ahead = scores(*steps[index + 1])
            if at < 0:
                shift = jnp.max(s, axis=0, keepdims=True) * SCALE2
            p = jnp.exp2(s * SCALE2 - shift)
            values = (
                nvt_ref[cols_of(h), :]
                if at < 0
                else cvt_ref[cols_of(h), at * CHUNK : (at + 1) * CHUNK]
            )
            more = dot(values, p.astype(BF16))
            total = jnp.sum(p, axis=0, keepdims=True) + (0.0 if at < 0 else total)
            o = more if at < 0 else o + more
            if at == chunks - 1:
                ot_s[h] = o * (1.0 / total)
                lse_s[h] = jnp.broadcast_to(shift + jnp.log2(total), (8, wide))
                tot_s[h] = jnp.broadcast_to(total, (8, wide))

    if looped:
        pl.loop(0, groups)(lambda h: sequence([h]))
    else:
        sequence(range(groups))

    fits = jnp.min(jnp.where(tot_s[...] <= LARGE, 1.0, 0.0))

    @pl.when(fits < 0.5)
    def _():
        def careful(h, _):
            cols = cols_of(h)
            q = q_s[:, cols]
            s_new = dot(nk_ref[:, cols], q, NT)

            def chunk_at(j):
                return pl.ds(pl.multiple_of(j * HD, HD), HD)

            def peak_of(j, peak):
                s = dot(ck_ref[chunk_at(j), cols], q, NT)
                return jnp.maximum(peak, jnp.max(s, axis=0, keepdims=True))

            turns = ck_ref.shape[0] // HD
            peak = lax.fori_loop(0, turns, peak_of, jnp.max(s_new, axis=0, keepdims=True))
            p = jnp.exp2((s_new - peak) * SCALE2)
            ot_s[h] = dot(nvt_ref[cols, :], p.astype(BF16))

            def add(j, total):
                s = dot(ck_ref[chunk_at(j), cols], q, NT)
                p = jnp.exp2((s - peak) * SCALE2)
                ot_s[h] += dot(cvt_ref[cols, chunk_at(j)], p.astype(BF16))
                return total + jnp.sum(p, axis=0, keepdims=True)

            total = lax.fori_loop(0, turns, add, jnp.sum(p, axis=0, keepdims=True))
            ot_s[h] = ot_s[h] * (1.0 / total)
            lse_s[h] = jnp.broadcast_to(peak * SCALE2 + jnp.log2(total), (8, wide))
            return 0

        lax.fori_loop(0, groups, careful, 0)

    each = rows + TAIL
    if oth_ref.shape[0] > count * each:
        oth_ref[count * each :] = more_ref[...]
    for h in range(groups):
        cols = slice(h * HD, (h + 1) * HD)
        o = ot_s[h].T.astype(BF16)
        lse = lse_s[h]
        for at, ref in enumerate(own_refs):
            for side, (to, base) in enumerate(((ref, 0), (oth_ref, at * each))):
                begin = at * pair + side * rows
                to[base : base + rows, cols] = o[begin : begin + rows]
                turned = pltpu.roll(lse, wide - begin, axis=1) if begin else lse
                to[base + rows : base + each, cols] = lse_rows(turned[0:1, :HD])


def attend(blocks, ck, nk, cvt, nvt, more=None, after=None, looped=False):
    count = len(blocks)
    pair, width = blocks[0].shape
    wide = -(-count * pair // HD) * HD
    groups = width // HD
    keys = ck.shape[0] + nk.shape[0]
    each = pair // 2 + TAIL
    extra = 0 if more is None else more.shape[0]
    last = (after if more is None else more, ANY if more is None else VMEM)
    return pl.pallas_call(
        functools.partial(attend_kernel, count, looped),
        in_specs=[VMEM] * (count + 4) + [last[1]],
        out_specs=[VMEM] * (count + 1),
        out_shape=[jax.ShapeDtypeStruct((each, width), BF16)] * count
        + [jax.ShapeDtypeStruct((count * each + extra, width), BF16)],
        scratch_shapes=[
            pltpu.VMEM((wide, width), BF16),
            pltpu.VMEM((groups, HD, wide), F32),
            pltpu.VMEM((groups, 8, wide), F32),
            pltpu.VMEM((groups, 8, wide), F32),
        ],
        compiler_params=pltpu.CompilerParams(vmem_limit_bytes=24 * MIB),
        cost_estimate=pl.CostEstimate(
            flops=12 * wide * keys * width, bytes_accessed=10**6, transcendentals=0
        ),
    )(*blocks, ck, nk, cvt, nvt, last[0])


def merged_heads(blocks):
    rows = blocks[0].shape[0] - TAIL
    groups = blocks[0].shape[1] // HD
    lses = [lse_of(block[rows:]) for block in blocks]
    high = functools.reduce(jnp.maximum, lses)
    weights = [jnp.exp2(lse - high) for lse in lses]
    total = functools.reduce(jnp.add, weights)
    lse = high + jnp.log2(total)
    packed = [weight / total for weight in weights]
    packed = [share[:, h * HD : (h + 1) * HD] for share in packed for h in range(groups)]
    square = jnp.concatenate(packed + [jnp.zeros((HD - len(packed), HD), F32)], axis=0).T
    for h in range(groups):
        cols = slice(h * HD, (h + 1) * HD)
        merged = 0.0
        for at, block in enumerate(blocks):
            column = at * groups + h
            merged += square[:rows, column : column + 1] * block[:rows, cols].astype(F32)
        yield cols, merged, lse[:, cols]


def merge_kernel(*refs):
    out_ref = refs[-1]
    rows = out_ref.shape[0] - TAIL
    for cols, merged, lse in merged_heads([ref[...] for ref in refs[:-1]]):
        out_ref[:rows, cols] = merged.astype(BF16)
        out_ref[rows:, cols] = lse_rows(lse)


def across_kernel(count, *refs):
    mine, theirs_ref, outs = refs[:count], refs[count], refs[count + 1 :]
    each = outs[0].shape[0]
    for at, (mine_ref, out_ref) in enumerate(zip(mine, outs)):
        for cols, merged, lse in merged_heads(
            [mine_ref[...], theirs_ref[at * each : (at + 1) * each]]
        ):
            out_ref[: each - TAIL, cols] = merged.astype(BF16)
            out_ref[each - TAIL :, cols] = lse_rows(lse)


def last_kernel(*refs):
    for cols, merged, _ in merged_heads([ref[...] for ref in refs[:-1]]):
        refs[-1][:, cols] = merged.astype(BF16)


def small(kernel, out_shape, *operands):
    return pl.pallas_call(
        kernel,
        out_shape=out_shape,
        compiler_params=pltpu.CompilerParams(vmem_limit_bytes=6 * MIB),
        cost_estimate=pl.CostEstimate(flops=1, bytes_accessed=1, transcendentals=0),
    )(*operands)


def ready_kernel(q_in, ck_in, nk_in, cv_in, nv_in, q_ref, ck_ref, nk_ref, cvt_ref, nvt_ref, cv_s, nv_s, sems):
    chunks = cv_in.shape[0] // CHUNK
    parts = [pl.ds(at * CHUNK, CHUNK) for at in range(chunks)]
    moves = [(cv_in.at[part], cv_s.at[part]) for part in parts]
    moves += [(nv_in, nv_s), (ck_in, ck_ref), (nk_in, nk_ref), (q_in, q_ref)]
    copies = [pltpu.make_async_copy(a, b, sems.at[at]) for at, (a, b) in enumerate(moves)]
    for copy in copies:
        copy.start()
    for at in range(chunks):
        copies[at].wait()
        @pl.loop(0, cv_in.shape[1] // HD)
        def _(h):
            cols = pl.ds(pl.multiple_of(h * HD, HD), HD)
            cvt_ref[cols, at * CHUNK : (at + 1) * CHUNK] = cv_s[at * CHUNK : (at + 1) * CHUNK, cols].T

    copies[chunks].wait()
    for h in range(cv_in.shape[1] // HD):
        cols = slice(h * HD, (h + 1) * HD)
        nvt_ref[cols, :] = nv_s[:, cols].T
    for copy in copies[chunks + 1 :]:
        copy.wait()


def ready(q, ck, nk, cv, nv):
    shapes = [q.shape, ck.shape, nk.shape, cv.shape[::-1], nv.shape[::-1]]
    return pl.pallas_call(
        ready_kernel,
        in_specs=[HBM] * 5,
        out_specs=[VMEM] * 5,
        out_shape=[jax.ShapeDtypeStruct(shape, BF16) for shape in shapes],
        scratch_shapes=[
            pltpu.VMEM(cv.shape, BF16),
            pltpu.VMEM(nv.shape, BF16),
            pltpu.SemaphoreType.DMA((cv.shape[0] // CHUNK + 4,)),
        ],
        compiler_params=pltpu.CompilerParams(vmem_limit_bytes=12 * MIB),
        cost_estimate=pl.CostEstimate(flops=0, bytes_accessed=7 * 10**6, transcendentals=0),
    )(*[pltpu.with_memory_space_constraint(array, pltpu.HBM) for array in (q, ck, nk, cv, nv)])


def pair_kernel(own_ref, oth_ref, _, out_ref):
    rows = own_ref.shape[0]
    out_ref[:rows] = own_ref[...]
    out_ref[rows:] = oth_ref[...]


def pair(own, oth, after):
    rows, width = own.shape
    return pl.pallas_call(
        pair_kernel,
        in_specs=[VMEM, VMEM, ANY],
        out_specs=VMEM,
        out_shape=jax.ShapeDtypeStruct((2 * rows, width), own.dtype),
        compiler_params=pltpu.CompilerParams(vmem_limit_bytes=4 * MIB),
    )(own, oth, after)


def gate_kernel(*refs):
    del refs


def gate(arrays, after, flops=0):
    count = len(arrays)
    return pl.pallas_call(
        gate_kernel,
        in_specs=[ANY] * (count + 1),
        out_specs=[ANY] * count,
        out_shape=[jax.ShapeDtypeStruct(array.shape, array.dtype) for array in arrays],
        input_output_aliases={at: at for at in range(count)},
        compiler_params=pltpu.CompilerParams(vmem_limit_bytes=MIB),
        cost_estimate=pl.CostEstimate(flops=flops, bytes_accessed=0, transcendentals=0),
    )(*arrays, after)


def arrange_kernel(y_ref, hi_ref, core_ref, own_ref, oth_ref, _, out_ref, sems):
    depth = own_ref.shape[0]
    block = own_ref.shape[1] // 16
    y, x_hi, core = y_ref[0], hi_ref[0], core_ref[0]

    def copy(at, side, ref):
        by, flip = at // 2, at % 2
        x_to = x_hi + flip - 2 * x_hi * flip
        first = (lax.rem(y + by, Y) * 4 + x_to * 2 + core) * block
        return pltpu.make_async_copy(
            ref.at[:, pl.ds(pl.multiple_of(first, HD), block)],
            out_ref.at[pl.ds(side * depth, depth), pl.ds(at * block, block)],
            sems.at[2 * at + side],
        )

    copies = [copy(at, side, ref) for at in range(8) for side, ref in enumerate((own_ref, oth_ref))]
    for one in copies:
        one.start()
    for one in copies:
        one.wait()


def arrange(own, oth, y, x_hi, core, after):
    depth, wide = own.shape
    smem = pl.BlockSpec(memory_space=pltpu.SMEM)
    return pl.pallas_call(
        arrange_kernel,
        in_specs=[smem, smem, smem, ANY, ANY, ANY],
        out_specs=VMEM,
        out_shape=jax.ShapeDtypeStruct((2 * depth, wide // 2), own.dtype),
        scratch_shapes=[pltpu.SemaphoreType.DMA((16,))],
        compiler_params=pltpu.CompilerParams(vmem_limit_bytes=8 * MIB),
        cost_estimate=pl.CostEstimate(flops=0, bytes_accessed=10**7, transcendentals=0),
    )(
        y.reshape(1),
        x_hi.reshape(1),
        core.reshape(1),
        pltpu.with_memory_space_constraint(own, pltpu.HBM),
        oth,
        after,
    )


def share_of(heads, weight_ref, by):
    return dot(heads, weight_ref[:, by * 6 * HD : (by + 1) * 6 * HD])


def both_of(own_ref, oth_ref):
    return jnp.concatenate([own_ref[...], oth_ref[...]], axis=1)


def far_kernel(own_ref, oth_ref, weight_ref, a_ref, b_ref):
    half = a_ref.shape[1]
    share = share_of(both_of(own_ref, oth_ref), weight_ref, 2)
    a_ref[...] = share[:, :half].astype(BF16)
    b_ref[...] = share[:, half:].astype(BF16)


def near_kernel(own_ref, oth_ref, weight_ref, up_ref, up_rest_ref, down_ref, down_rest_ref):
    half = up_ref.shape[1]
    heads = both_of(own_ref, oth_ref)
    share = share_of(heads, weight_ref, 1)
    up_ref[...] = share[:, :half]
    up_rest_ref[...] = share[:, half:].astype(BF16)
    share = share_of(heads, weight_ref, 3)
    down_ref[...] = share[:, :half].astype(BF16)
    down_rest_ref[...] = share[:, half:]


def here_kernel(own_ref, oth_ref, weight_ref, out_ref, rest_ref):
    half = out_ref.shape[1]
    share = share_of(both_of(own_ref, oth_ref), weight_ref, 0)
    out_ref[...] = share[:, :half]
    rest_ref[...] = share[:, half:]


def sum_kernel(*refs):
    total = refs[0][...].astype(F32)
    for ref in refs[1:-1]:
        total += ref[...].astype(F32)
    refs[-1][...] = total.astype(refs[-1].dtype)


def projecting(kernel, out_shape, *operands):
    rows, depth = operands[0].shape
    return pl.pallas_call(
        kernel,
        out_shape=out_shape,
        compiler_params=pltpu.CompilerParams(vmem_limit_bytes=14 * MIB),
        cost_estimate=pl.CostEstimate(
            flops=16 * rows * depth * depth, bytes_accessed=2 * 10**6, transcendentals=0
        ),
    )(*operands)


def body(queries, new_keys, new_values, cache_keys, cache_values, out_weight):
    rows, width = queries.shape
    head_at = lax.axis_index("head").astype(jnp.int32)
    core, x_hi, y = head_at & 1, (head_at >> 1) & 1, head_at >> 2

    def along_z(array, by):
        return lax.ppermute(
            array, "ctx", [(x * Z + z, x * Z + (z + by) % Z) for x in range(2) for z in range(Z)]
        )

    def across_x(array):
        return lax.ppermute(array, "ctx", [(i, (i + Z) % (2 * Z)) for i in range(2 * Z)])

    def across_core(array):
        return lax.ppermute(array, "head", [(i, i ^ 1) for i in range(4 * Y)])

    def across_hi(array):
        return lax.ppermute(array, "head", [(i, i ^ 2) for i in range(4 * Y)])

    def along_y(array, by):
        return lax.ppermute(array, "head", [(i, (i + 4 * by) % (4 * Y)) for i in range(4 * Y)])

    def shape(*dims, dtype=BF16):
        return jax.ShapeDtypeStruct(dims, dtype)

    weight_oth = across_core(out_weight)
    q_here, *cached = ready(queries, cache_keys, new_keys, cache_values, new_values)
    q = {0: pair(q_here, across_x(queries), cached[0])}
    q[1], q[-1] = along_z(q[0], -1), along_z(q[0], 1)
    part = {}
    part[0], oth = attend([q[0]], *cached, after=q_here, looped=True)
    ahead = [along_z(q[1], -1), along_z(q[-1], 1)]
    part[1], part[-1], oth = attend([q[1], q[-1]], *cached, more=oth)
    q[2], q[-2] = gate(ahead, part[1])
    ahead = [along_z(q[2], -1), along_z(q[-2], 1)]
    part[2], part[-2], near = attend([q[2], q[-2]], *cached, after=part[1])
    q[3], q[-3] = gate(ahead, part[2])
    ahead = along_z(q[3], -1)
    oth = across_x(gate([oth], q[2])[0])
    part[3], part[-3], far = attend([q[3], q[-3]], *cached, after=oth)
    (q[4],) = gate([ahead], part[3])
    near = across_x(gate([near], q[3])[0])
    part[4], last = attend([q[4]], *cached, after=near)

    one = shape(rows + TAIL, width)

    def merged(theirs, *blocks):
        out = small(
            functools.partial(across_kernel, len(blocks)),
            [one] * len(blocks),
            *[part[d] for d in blocks],
            theirs,
        )
        part.update(zip(blocks, out))

    def met(there, here):
        return small(merge_kernel, one, there, here)

    far = across_x(gate([far], last)[0])
    merged(gate([across_x(last)], part[0], flops=2 * 10**9)[0], 4)
    merged(gate([far], part[4])[0], 3, -3)
    merged(gate([near], part[3])[0], 2, -2)
    merged(gate([oth], part[2])[0], 1, -1, 0)
    up = met(along_z(part[4], 1), part[3])
    down = met(gate([along_z(part[-3], -1)], up)[0], part[-2])
    close = met(gate([along_z(part[2], 1)], down)[0], part[1])
    weight = arrange(out_weight, weight_oth, y, x_hi, core, close)
    (up,) = gate([along_z(up, 3)], weight, flops=10**10)
    back = [along_z(part[-1], -1), along_z(close, 1), along_z(down, -2), up]
    own = small(last_kernel, shape(rows, width), part[0], *back)

    oth = across_core(own)
    tile, wide = shape(rows, width), shape(rows, width, dtype=F32)
    a, b = projecting(far_kernel, [tile, tile], own, oth, weight)
    b, a = along_y(b, -1), along_y(a, 1)
    up, up_rest, down, down_rest = projecting(near_kernel, [wide, tile, tile, wide], own, oth, weight)
    (b,) = gate([b], up, flops=10**10)
    (up_rest,) = gate([along_y(up_rest, 1)], b, flops=2 * 10**10)
    down_rest = small(sum_kernel, tile, down_rest, b)
    down = along_y(gate([down], down_rest)[0], -1)
    (a,) = gate([a], down_rest, flops=2 * 10**10)
    down_rest = along_y(down_rest, -1)
    up = along_y(small(sum_kernel, tile, up, a), 1)
    here, rest = projecting(here_kernel, [wide, wide], own, oth, weight)
    (down_rest,) = gate([down_rest], here, flops=4 * 10**10)
    rest = across_hi(small(sum_kernel, tile, rest, up_rest, down_rest))
    ours = small(sum_kernel, wide, here, up, down)
    return ours + rest.astype(F32)


def solution(mesh):
    placed = (
        P("ctx", "head"),
        P("ctx", "head"),
        P("ctx", "head"),
        P("ctx", "head"),
        P("ctx", "head"),
        P("head", None),
    )
    return jax.shard_map(
        body, mesh=mesh, in_specs=placed, out_specs=P("ctx", "head"), check_vma=False
    )
```

```python
import functools

import jax
import jax.numpy as jnp
from jax import lax
from jax.experimental import pallas as pl
from jax.experimental.pallas import tpu as pltpu
from jax.sharding import PartitionSpec as P

HD = 128
SCALE2 = HD ** (-0.5) * 1.4426950408889634
CHUNK = 512
TAIL = 16
LARGE = 2.0**100
MIB = 1024 * 1024
Z, Y = 8, 4
NT = (((1,), (1,)), ((), ()))
F32 = jnp.float32
BF16 = jnp.bfloat16
VMEM = pl.BlockSpec(memory_space=pltpu.VMEM)
ANY = pl.BlockSpec(memory_space=pl.ANY)
HBM = pl.BlockSpec(memory_space=pltpu.HBM)


def dot(a, b, dims=(((1,), (0,)), ((), ()))):
    return lax.dot_general(a, b, dims, preferred_element_type=F32)


def lse_rows(lse):
    at = lax.broadcasted_iota(jnp.int32, (8, HD), 0)
    row = jnp.broadcast_to(lse, (8, HD))
    hi = row.astype(BF16).astype(F32)
    mid = (row - hi).astype(BF16).astype(F32)
    out = jnp.where(at == 0, hi, jnp.where(at == 1, mid, jnp.where(at == 2, row - hi - mid, 0.0)))
    return jnp.concatenate([out, jnp.zeros((TAIL - 8, HD), F32)], axis=0).astype(BF16)


def lse_of(tail):
    parts = tail[0:3].astype(F32)
    return parts[0:1] + parts[1:2] + parts[2:3]


def attend_kernel(count, looped, *refs):
    q_refs, refs = refs[:count], refs[count:]
    ck_ref, nk_ref, cvt_ref, nvt_ref, more_ref = refs[:5]
    own_refs, oth_ref = refs[5 : 5 + count], refs[5 + count]
    q_s, ot_s, lse_s, tot_s = refs[6 + count :]
    pair = q_refs[0].shape[0]
    rows = pair // 2
    wide = q_s.shape[0]
    groups = ck_ref.shape[1] // HD
    chunks = ck_ref.shape[0] // CHUNK
    for at, ref in enumerate(q_refs):
        q_s[at * pair : (at + 1) * pair] = ref[...]
    if wide > count * pair:
        q_s[count * pair :] = jnp.zeros((wide - count * pair, q_s.shape[1]), BF16)

    def cols_of(h):
        if isinstance(h, int):
            return slice(h * HD, (h + 1) * HD)
        return pl.ds(pl.multiple_of(h * HD, HD), HD)

    def sequence(heads):
        steps = [(h, at) for h in heads for at in range(-1, chunks)]

        def scores(h, at):
            keys = nk_ref[:, cols_of(h)] if at < 0 else ck_ref[at * CHUNK : (at + 1) * CHUNK, cols_of(h)]
            return dot(keys, q_s[:, cols_of(h)], NT)

        ahead = scores(*steps[0])
        for index, (h, at) in enumerate(steps):
            s = ahead
            if index + 1 < len(steps):
                ahead = scores(*steps[index + 1])
            if at < 0:
                shift = jnp.max(s, axis=0, keepdims=True) * SCALE2
            p = jnp.exp2(s * SCALE2 - shift)
            values = (
                nvt_ref[cols_of(h), :]
                if at < 0
                else cvt_ref[cols_of(h), at * CHUNK : (at + 1) * CHUNK]
            )
            more = dot(values, p.astype(BF16))
            total = jnp.sum(p, axis=0, keepdims=True) + (0.0 if at < 0 else total)
            o = more if at < 0 else o + more
            if at == chunks - 1:
                ot_s[h] = o * (1.0 / total)
                lse_s[h] = jnp.broadcast_to(shift + jnp.log2(total), (8, wide))
                tot_s[h] = jnp.broadcast_to(total, (8, wide))

    if looped:
        pl.loop(0, groups)(lambda h: sequence([h]))
    else:
        sequence(range(groups))

    fits = jnp.min(jnp.where(tot_s[...] <= LARGE, 1.0, 0.0))

    @pl.when(fits < 0.5)
    def _():
        def careful(h, _):
            cols = cols_of(h)
            q = q_s[:, cols]
            s_new = dot(nk_ref[:, cols], q, NT)

            def chunk_at(j):
                return pl.ds(pl.multiple_of(j * HD, HD), HD)

            def peak_of(j, peak):
                s = dot(ck_ref[chunk_at(j), cols], q, NT)
                return jnp.maximum(peak, jnp.max(s, axis=0, keepdims=True))

            turns = ck_ref.shape[0] // HD
            peak = lax.fori_loop(0, turns, peak_of, jnp.max(s_new, axis=0, keepdims=True))
            p = jnp.exp2((s_new - peak) * SCALE2)
            ot_s[h] = dot(nvt_ref[cols, :], p.astype(BF16))

            def add(j, total):
                s = dot(ck_ref[chunk_at(j), cols], q, NT)
                p = jnp.exp2((s - peak) * SCALE2)
                ot_s[h] += dot(cvt_ref[cols, chunk_at(j)], p.astype(BF16))
                return total + jnp.sum(p, axis=0, keepdims=True)

            total = lax.fori_loop(0, turns, add, jnp.sum(p, axis=0, keepdims=True))
            ot_s[h] = ot_s[h] * (1.0 / total)
            lse_s[h] = jnp.broadcast_to(peak * SCALE2 + jnp.log2(total), (8, wide))
            return 0

        lax.fori_loop(0, groups, careful, 0)

    each = rows + TAIL
    if oth_ref.shape[0] > count * each:
        oth_ref[count * each :] = more_ref[...]
    for h in range(groups):
        cols = slice(h * HD, (h + 1) * HD)
        o = ot_s[h].T.astype(BF16)
        lse = lse_s[h]
        for at, ref in enumerate(own_refs):
            for side, (to, base) in enumerate(((ref, 0), (oth_ref, at * each))):
                begin = at * pair + side * rows
                to[base : base + rows, cols] = o[begin : begin + rows]
                turned = pltpu.roll(lse, wide - begin, axis=1) if begin else lse
                to[base + rows : base + each, cols] = lse_rows(turned[0:1, :HD])


def attend(blocks, ck, nk, cvt, nvt, more=None, after=None, looped=False):
    count = len(blocks)
    pair, width = blocks[0].shape
    wide = -(-count * pair // HD) * HD
    groups = width // HD
    keys = ck.shape[0] + nk.shape[0]
    each = pair // 2 + TAIL
    extra = 0 if more is None else more.shape[0]
    last = (after if more is None else more, ANY if more is None else VMEM)
    return pl.pallas_call(
        functools.partial(attend_kernel, count, looped),
        in_specs=[VMEM] * (count + 4) + [last[1]],
        out_specs=[VMEM] * (count + 1),
        out_shape=[jax.ShapeDtypeStruct((each, width), BF16)] * count
        + [jax.ShapeDtypeStruct((count * each + extra, width), BF16)],
        scratch_shapes=[
            pltpu.VMEM((wide, width), BF16),
            pltpu.VMEM((groups, HD, wide), F32),
            pltpu.VMEM((groups, 8, wide), F32),
            pltpu.VMEM((groups, 8, wide), F32),
        ],
        compiler_params=pltpu.CompilerParams(vmem_limit_bytes=24 * MIB),
        cost_estimate=pl.CostEstimate(
            flops=12 * wide * keys * width, bytes_accessed=10**6, transcendentals=0
        ),
    )(*blocks, ck, nk, cvt, nvt, last[0])


def merged_heads(blocks):
    rows = blocks[0].shape[0] - TAIL
    groups = blocks[0].shape[1] // HD
    lses = [lse_of(block[rows:]) for block in blocks]
    high = functools.reduce(jnp.maximum, lses)
    weights = [jnp.exp2(lse - high) for lse in lses]
    total = functools.reduce(jnp.add, weights)
    lse = high + jnp.log2(total)
    packed = [weight / total for weight in weights]
    packed = [share[:, h * HD : (h + 1) * HD] for share in packed for h in range(groups)]
    square = jnp.concatenate(packed + [jnp.zeros((HD - len(packed), HD), F32)], axis=0).T
    for h in range(groups):
        cols = slice(h * HD, (h + 1) * HD)
        merged = 0.0
        for at, block in enumerate(blocks):
            column = at * groups + h
            merged += square[:rows, column : column + 1] * block[:rows, cols].astype(F32)
        yield cols, merged, lse[:, cols]


def merge_kernel(*refs):
    out_ref = refs[-1]
    rows = out_ref.shape[0] - TAIL
    for cols, merged, lse in merged_heads([ref[...] for ref in refs[:-1]]):
        out_ref[:rows, cols] = merged.astype(BF16)
        out_ref[rows:, cols] = lse_rows(lse)


def across_kernel(count, *refs):
    mine, theirs_ref, outs = refs[:count], refs[count], refs[count + 1 :]
    each = outs[0].shape[0]
    for at, (mine_ref, out_ref) in enumerate(zip(mine, outs)):
        for cols, merged, lse in merged_heads(
            [mine_ref[...], theirs_ref[at * each : (at + 1) * each]]
        ):
            out_ref[: each - TAIL, cols] = merged.astype(BF16)
            out_ref[each - TAIL :, cols] = lse_rows(lse)


def last_kernel(*refs):
    for cols, merged, _ in merged_heads([ref[...] for ref in refs[:-1]]):
        refs[-1][:, cols] = merged.astype(BF16)


def small(kernel, out_shape, *operands):
    return pl.pallas_call(
        kernel,
        out_shape=out_shape,
        compiler_params=pltpu.CompilerParams(vmem_limit_bytes=6 * MIB),
        cost_estimate=pl.CostEstimate(flops=1, bytes_accessed=1, transcendentals=0),
    )(*operands)


def ready_kernel(q_in, ck_in, nk_in, cv_in, nv_in, q_ref, ck_ref, nk_ref, cvt_ref, nvt_ref, cv_s, nv_s, sems):
    chunks = cv_in.shape[0] // CHUNK
    parts = [pl.ds(at * CHUNK, CHUNK) for at in range(chunks)]
    moves = [(cv_in.at[part], cv_s.at[part]) for part in parts]
    moves += [(nv_in, nv_s), (ck_in, ck_ref), (nk_in, nk_ref), (q_in, q_ref)]
    copies = [pltpu.make_async_copy(a, b, sems.at[at]) for at, (a, b) in enumerate(moves)]
    for copy in copies:
        copy.start()
    for at in range(chunks):
        copies[at].wait()
        @pl.loop(0, cv_in.shape[1] // HD)
        def _(h):
            cols = pl.ds(pl.multiple_of(h * HD, HD), HD)
            cvt_ref[cols, at * CHUNK : (at + 1) * CHUNK] = cv_s[at * CHUNK : (at + 1) * CHUNK, cols].T

    copies[chunks].wait()
    for h in range(cv_in.shape[1] // HD):
        cols = slice(h * HD, (h + 1) * HD)
        nvt_ref[cols, :] = nv_s[:, cols].T
    for copy in copies[chunks + 1 :]:
        copy.wait()


def ready(q, ck, nk, cv, nv):
    shapes = [q.shape, ck.shape, nk.shape, cv.shape[::-1], nv.shape[::-1]]
    return pl.pallas_call(
        ready_kernel,
        in_specs=[HBM] * 5,
        out_specs=[VMEM] * 5,
        out_shape=[jax.ShapeDtypeStruct(shape, BF16) for shape in shapes],
        scratch_shapes=[
            pltpu.VMEM(cv.shape, BF16),
            pltpu.VMEM(nv.shape, BF16),
            pltpu.SemaphoreType.DMA((cv.shape[0] // CHUNK + 4,)),
        ],
        compiler_params=pltpu.CompilerParams(vmem_limit_bytes=12 * MIB),
        cost_estimate=pl.CostEstimate(flops=0, bytes_accessed=7 * 10**6, transcendentals=0),
    )(*[pltpu.with_memory_space_constraint(array, pltpu.HBM) for array in (q, ck, nk, cv, nv)])


def pair_kernel(own_ref, oth_ref, _, out_ref):
    rows = own_ref.shape[0]
    out_ref[:rows] = own_ref[...]
    out_ref[rows:] = oth_ref[...]


def pair(own, oth, after):
    rows, width = own.shape
    return pl.pallas_call(
        pair_kernel,
        in_specs=[VMEM, VMEM, ANY],
        out_specs=VMEM,
        out_shape=jax.ShapeDtypeStruct((2 * rows, width), own.dtype),
        compiler_params=pltpu.CompilerParams(vmem_limit_bytes=4 * MIB),
    )(own, oth, after)


def gate_kernel(*refs):
    del refs


def gate(arrays, after, flops=0):
    count = len(arrays)
    return pl.pallas_call(
        gate_kernel,
        in_specs=[ANY] * (count + 1),
        out_specs=[ANY] * count,
        out_shape=[jax.ShapeDtypeStruct(array.shape, array.dtype) for array in arrays],
        input_output_aliases={at: at for at in range(count)},
        compiler_params=pltpu.CompilerParams(vmem_limit_bytes=MIB),
        cost_estimate=pl.CostEstimate(flops=flops, bytes_accessed=0, transcendentals=0),
    )(*arrays, after)


def arrange_kernel(y_ref, hi_ref, core_ref, own_ref, oth_ref, _, out_ref, sems):
    depth = own_ref.shape[0]
    block = own_ref.shape[1] // 16
    y, x_hi, core = y_ref[0], hi_ref[0], core_ref[0]

    def copy(at, side, ref):
        by, flip = at // 2, at % 2
        x_to = x_hi + flip - 2 * x_hi * flip
        first = (lax.rem(y + by, Y) * 4 + x_to * 2 + core) * block
        return pltpu.make_async_copy(
            ref.at[:, pl.ds(pl.multiple_of(first, HD), block)],
            out_ref.at[pl.ds(side * depth, depth), pl.ds(at * block, block)],
            sems.at[2 * at + side],
        )

    copies = [copy(at, side, ref) for at in range(8) for side, ref in enumerate((own_ref, oth_ref))]
    for one in copies:
        one.start()
    for one in copies:
        one.wait()


def arrange(own, oth, y, x_hi, core, after):
    depth, wide = own.shape
    smem = pl.BlockSpec(memory_space=pltpu.SMEM)
    return pl.pallas_call(
        arrange_kernel,
        in_specs=[smem, smem, smem, ANY, ANY, ANY],
        out_specs=VMEM,
        out_shape=jax.ShapeDtypeStruct((2 * depth, wide // 2), own.dtype),
        scratch_shapes=[pltpu.SemaphoreType.DMA((16,))],
        compiler_params=pltpu.CompilerParams(vmem_limit_bytes=8 * MIB),
        cost_estimate=pl.CostEstimate(flops=0, bytes_accessed=10**7, transcendentals=0),
    )(
        y.reshape(1),
        x_hi.reshape(1),
        core.reshape(1),
        pltpu.with_memory_space_constraint(own, pltpu.HBM),
        oth,
        after,
    )


def share_of(heads, weight_ref, by):
    return dot(heads, weight_ref[:, by * 6 * HD : (by + 1) * 6 * HD])


def both_of(own_ref, oth_ref):
    return jnp.concatenate([own_ref[...], oth_ref[...]], axis=1)


def far_kernel(own_ref, oth_ref, weight_ref, a_ref, b_ref):
    half = a_ref.shape[1]
    share = share_of(both_of(own_ref, oth_ref), weight_ref, 2)
    a_ref[...] = share[:, :half].astype(BF16)
    b_ref[...] = share[:, half:].astype(BF16)


def near_kernel(own_ref, oth_ref, weight_ref, up_ref, up_rest_ref, down_ref, down_rest_ref):
    half = up_ref.shape[1]
    heads = both_of(own_ref, oth_ref)
    share = share_of(heads, weight_ref, 1)
    up_ref[...] = share[:, :half]
    up_rest_ref[...] = share[:, half:].astype(BF16)
    share = share_of(heads, weight_ref, 3)
    down_ref[...] = share[:, :half].astype(BF16)
    down_rest_ref[...] = share[:, half:]


def here_kernel(own_ref, oth_ref, weight_ref, out_ref, rest_ref):
    half = out_ref.shape[1]
    share = share_of(both_of(own_ref, oth_ref), weight_ref, 0)
    out_ref[...] = share[:, :half]
    rest_ref[...] = share[:, half:]


def sum_kernel(*refs):
    total = refs[0][...].astype(F32)
    for ref in refs[1:-1]:
        total += ref[...].astype(F32)
    refs[-1][...] = total.astype(refs[-1].dtype)


def projecting(kernel, out_shape, *operands):
    rows, depth = operands[0].shape
    return pl.pallas_call(
        kernel,
        out_shape=out_shape,
        compiler_params=pltpu.CompilerParams(vmem_limit_bytes=14 * MIB),
        cost_estimate=pl.CostEstimate(
            flops=16 * rows * depth * depth, bytes_accessed=2 * 10**6, transcendentals=0
        ),
    )(*operands)


def body(queries, new_keys, new_values, cache_keys, cache_values, out_weight):
    rows, width = queries.shape
    head_at = lax.axis_index("head").astype(jnp.int32)
    core, x_hi, y = head_at & 1, (head_at >> 1) & 1, head_at >> 2

    def along_z(array, by):
        return lax.ppermute(
            array, "ctx", [(x * Z + z, x * Z + (z + by) % Z) for x in range(2) for z in range(Z)]
        )

    def across_x(array):
        return lax.ppermute(array, "ctx", [(i, (i + Z) % (2 * Z)) for i in range(2 * Z)])

    def across_core(array):
        return lax.ppermute(array, "head", [(i, i ^ 1) for i in range(4 * Y)])

    def across_hi(array):
        return lax.ppermute(array, "head", [(i, i ^ 2) for i in range(4 * Y)])

    def along_y(array, by):
        return lax.ppermute(array, "head", [(i, (i + 4 * by) % (4 * Y)) for i in range(4 * Y)])

    def shape(*dims, dtype=BF16):
        return jax.ShapeDtypeStruct(dims, dtype)

    weight_oth = across_core(out_weight)
    q_here, *cached = ready(queries, cache_keys, new_keys, cache_values, new_values)
    q = {0: pair(q_here, across_x(queries), cached[0])}
    q[1], q[-1] = along_z(q[0], -1), along_z(q[0], 1)
    part = {}
    part[0], oth = attend([q[0]], *cached, after=q_here, looped=True)
    ahead = [along_z(q[1], -1), along_z(q[-1], 1)]
    part[1], part[-1], oth = attend([q[1], q[-1]], *cached, more=oth)
    q[2], q[-2] = gate(ahead, part[1])
    ahead = [along_z(q[2], -1), along_z(q[-2], 1)]
    part[2], part[-2], near = attend([q[2], q[-2]], *cached, after=part[1])
    q[3], q[-3] = gate(ahead, part[2])
    ahead = along_z(q[3], -1)
    part[3], part[-3], far = attend([q[3], q[-3]], *cached, after=part[2])
    (q[4],) = gate([ahead], part[3])
    part[4], last = attend([q[4]], *cached, after=part[3])

    one = shape(rows + TAIL, width)

    def merged(theirs, *blocks):
        out = small(
            functools.partial(across_kernel, len(blocks)),
            [one] * len(blocks),
            *[part[d] for d in blocks],
            theirs,
        )
        part.update(zip(blocks, out))

    def met(there, here):
        return small(merge_kernel, one, there, here)

    oth = across_x(gate([oth], q[2])[0])
    near = across_x(gate([near], q[3])[0])
    far = across_x(gate([far], q[4])[0])
    weight = arrange(out_weight, weight_oth, y, x_hi, core, last)
    merged(gate([across_x(last)], weight)[0], 4)
    merged(gate([far], part[4])[0], 3, -3)
    merged(gate([near], part[3])[0], 2, -2)
    merged(gate([oth], part[2])[0], 1, -1, 0)
    up = met(along_z(part[4], 1), part[3])
    down = met(gate([along_z(part[-3], -1)], up)[0], part[-2])
    close = met(gate([along_z(part[2], 1)], down)[0], part[1])
    (up,) = gate([along_z(up, 3)], part[0], flops=10**10)
    back = [along_z(part[-1], -1), along_z(close, 1), along_z(down, -2), up]
    own = small(last_kernel, shape(rows, width), part[0], *back)

    oth = across_core(own)
    tile, wide = shape(rows, width), shape(rows, width, dtype=F32)
    a, b = projecting(far_kernel, [tile, tile], own, oth, weight)
    b, a = along_y(b, -1), along_y(a, 1)
    up, up_rest, down, down_rest = projecting(near_kernel, [wide, tile, tile, wide], own, oth, weight)
    (b,) = gate([b], up, flops=10**10)
    (up_rest,) = gate([along_y(up_rest, 1)], b, flops=2 * 10**10)
    down_rest = small(sum_kernel, tile, down_rest, b)
    down = along_y(gate([down], down_rest)[0], -1)
    (a,) = gate([a], down_rest, flops=2 * 10**10)
    down_rest = along_y(down_rest, -1)
    up = along_y(small(sum_kernel, tile, up, a), 1)
    here, rest = projecting(here_kernel, [wide, wide], own, oth, weight)
    (down_rest,) = gate([down_rest], here, flops=4 * 10**10)
    rest = across_hi(small(sum_kernel, tile, rest, up_rest, down_rest))
    ours = small(sum_kernel, wide, here, up, down)
    return ours + rest.astype(F32)


def solution(mesh):
    placed = (
        P("ctx", "head"),
        P("ctx", "head"),
        P("ctx", "head"),
        P("ctx", "head"),
        P("ctx", "head"),
        P("head", None),
    )
    return jax.shard_map(
        body, mesh=mesh, in_specs=placed, out_specs=P("ctx", "head"), check_vma=False
    )
```
